512 devices in a mesh: tm: 64 (over y, x, core), chan: 8 (over z).
Axes of the slice: x: 4, y: 8, z: 8, core: 2. Of those that a mesh axis runs over, the one named last changes fastest.
Arguments:
- frames: bfloat16 [64, 512, 1024], P('tm', 'chan'), may hold values from -6 to 6
- decay_rate: float32 [256], P('chan'), may hold values from 0.003125 to 0.1
- step_size: float32 [64], P('tm'), may hold values from 0.5 to 103.9
- in_kernel: bfloat16 [9, 256, 512], replicated, may hold values from -0.09375 to 0.09375
- out_kernel: bfloat16 [9, 512, 256], P(None, 'chan'), may hold values from -0.125 to 0.125
- skip_gain: float32 [512], P('chan'), may hold values from 0.5 to 1.5
Outputs:
- outputs: bfloat16 [64, 512, 1024], P('tm', 'chan')
The draws below stay inside these ranges and needn't reach their ends.
All inputs are finite; a program needn't handle non-finite values.
Results may differ from the reference program's by a relative error of at most 0.013.
Values may be sent and summed in bfloat16 or wider, within the bound.
No kernel may reach another device: no remote copies, remote signals or barrier semaphores. Data moves between devices by JAX's collectives and lax.ppermute only.
A program may use at most 64 MiB of HBM per device.

```python
import jax
import jax.numpy as jnp
from jax import lax

U = 512
P_SIZE = 256
GRID_W = 32
CELLS = 1024
FRAMES = 64


def draw_decay_rate(key, part):
    key = jax.random.fold_in(key, 11)
    lowest = jnp.log(0.2 / FRAMES)
    highest = jnp.log(0.1)
    spread = jax.random.uniform(key, (P_SIZE,), jnp.float32)
    return jnp.exp(lowest + (highest - lowest) * spread).astype(jnp.float32)


def draw_step_size(key, part):
    key = jax.random.fold_in(key, 23)
    first, second = jax.random.split(key)
    base = jax.random.uniform(first, (FRAMES,), jnp.float32, 0.5, 1.5)
    places = jax.random.randint(second, (2,), 0, FRAMES)
    hits = (jnp.arange(FRAMES)[None, :] == places[:, None]).astype(jnp.float32)
    return (base + 0.8 * FRAMES * jnp.sum(hits, axis=0)).astype(jnp.float32)


def shard_levels(stream_key, extent, cuts, low, top_value):
    level = 1.0
    for axis_at, parts in cuts:
        steps = jax.random.uniform(jax.random.fold_in(jax.random.fold_in(stream_key, 6), axis_at), (parts,), jnp.float32, low / len(cuts), top_value / len(cuts))
        level = level * jnp.repeat(jnp.exp(steps), extent[axis_at] // parts).reshape((-1,) + (1,) * (len(extent) - 1 - axis_at))
    return level


def centred(own_key, dims, width, bound, pieces=(), kind=jnp.bfloat16):
    level = shard_levels(own_key, dims, pieces, -0.22, 0.18) if pieces else 1.0
    drawn = jax.random.normal(own_key, dims, jnp.float32) * width * level
    return jnp.minimum(jnp.maximum(drawn, -bound), bound).astype(kind)


def setup_inputs(seed: int = 0) -> dict:
    splits = jax.random.split(jax.random.key(seed), 7)
    frames = centred(splits[0], (FRAMES, U, CELLS), 1.0, 6.0, ((0, 64), (1, 8)))
    decay_rate = draw_decay_rate(jax.random.fold_in(splits[6], 71), 0)
    step_size = draw_step_size(jax.random.fold_in(splits[6], 71), 0)
    in_kernel = centred(splits[3], (9, P_SIZE, U), (9 * U) ** -0.5, 0.09375)
    out_kernel = centred(splits[4], (9, U, P_SIZE), (9 * P_SIZE) ** -0.5, 0.125, ((1, 8),))
    skip_gain = jnp.clip(0.5 + 1.0 * jax.random.uniform(splits[5], (U,), jnp.float32) ** shard_levels(splits[5], (U,), ((0, 8),), -0.2, 0.2), 0.5, 1.5)
    return dict(frames=frames, decay_rate=decay_rate, step_size=step_size, in_kernel=in_kernel, out_kernel=out_kernel, skip_gain=skip_gain)


def shift_sum(stacked, axis, grid_w):
    cells = stacked.shape[-1]
    margin = grid_w + 1
    widths = [(0, 0)] * (stacked.ndim - 1) + [(margin, margin)]
    padded = jnp.pad(stacked, widths)
    column = jnp.arange(cells) % grid_w
    total = None
    for offset in range(9):
        row_step = offset // 3 - 1
        col_step = offset % 3 - 1
        begin_at = margin + row_step * grid_w + col_step
        taken = lax.index_in_dim(padded, offset, axis, keepdims=False)
        moved = taken[..., begin_at:begin_at + cells]
        inside = ((column + col_step >= 0) & (column + col_step < grid_w)).astype(moved.dtype)
        total = moved * inside if total is None else total + moved * inside
    return total

def reference(frames, decay_rate, step_size, in_kernel, out_kernel, skip_gain):
    in_flat = in_kernel.reshape(9 * P_SIZE, U)
    out_flat = out_kernel.reshape(9 * U, P_SIZE)

    def advance(state, inputs):
        frame, stride = inputs
        driven = shift_sum(jnp.dot(in_flat, frame, preferred_element_type=jnp.float32).reshape(9, P_SIZE, CELLS), 0, GRID_W)
        decay = jnp.exp(-decay_rate * stride)
        inject = jnp.sqrt(1.0 - decay * decay)
        state = decay[:, None] * state + inject[:, None] * driven
        rounded = state.astype(jnp.bfloat16)
        mixed = shift_sum(jnp.dot(out_flat, rounded, preferred_element_type=jnp.float32).reshape(9, U, CELLS), 0, GRID_W)
        mixed = mixed + skip_gain[:, None] * frame.astype(jnp.float32)
        return (state, jax.nn.gelu(mixed).astype(jnp.bfloat16))
    start = jnp.zeros((P_SIZE, CELLS), jnp.float32)
    final, outputs = lax.scan(advance, start, (frames, step_size))
    return outputs
```

```python
import functools

import jax
import jax.numpy as jnp
from jax import lax
from jax.experimental import pallas as pl
from jax.experimental.pallas import tpu as pltpu
from jax.sharding import Mesh, PartitionSpec as P

ROW = 32
TILE = 128
BF = jnp.bfloat16
F32 = jnp.float32


def lanes_of(shape):
    return lax.broadcasted_iota(jnp.int32, shape, len(shape) - 1)


def roll_lanes(x, by):
    return pltpu.roll(x, by % x.shape[-1], len(x.shape) - 1)


def to_column(row):
    n = row.shape[-1]
    eye = lax.broadcasted_iota(jnp.int32, (n, n), 0) == lax.broadcasted_iota(jnp.int32, (n, n), 1)
    return jnp.sum(jnp.where(eye, jnp.broadcast_to(row, (n, n)), 0.0), axis=1, keepdims=True)


def pieces(column):
    high = column.astype(BF).astype(F32)
    rest = column - high
    mid = rest.astype(BF).astype(F32)
    return high, mid, rest - mid


def spread(column, at, shape):
    lane = lanes_of(shape)
    tile = jnp.zeros(shape, F32)
    for n, piece in enumerate(pieces(column)):
        tile = jnp.where(lane == at + n, piece, tile)
    return tile


def collect(tile, at):
    lane = lanes_of(tile.shape)
    inside = (lane >= at) & (lane < at + 3)
    return jnp.sum(jnp.where(inside, tile.astype(F32), 0.0), axis=-1, keepdims=True)


def call(kernel, outs, *operands, smem=(), vmem=32):
    specs = [
        pl.BlockSpec(memory_space=pltpu.SMEM if n in smem else pltpu.VMEM) for n in range(len(operands))
    ]
    return pl.pallas_call(
        kernel,
        out_shape=outs,
        in_specs=specs,
        out_specs=pl.BlockSpec(memory_space=pltpu.VMEM),
        compiler_params=pltpu.CompilerParams(vmem_limit_bytes=vmem << 20),
    )(*operands)


def cut_rows(frame_ref, rate_ref, out_ref):
    blocks = out_ref.shape[0]
    channels = out_ref.shape[1]
    lane = lanes_of((channels, TILE))
    own = to_column(rate_ref[...])
    column = jnp.concatenate([own, jnp.zeros((channels - own.shape[0], 1), F32)], axis=0)
    meta = spread(column, ROW, (channels, TILE))
    for b in range(blocks):
        out_ref[b, :, :TILE] = frame_ref[:, b * TILE : (b + 1) * TILE]
        side = meta
        if b + 1 < blocks:
            after = frame_ref[:, (b + 1) * TILE : (b + 2) * TILE].astype(F32)
            side = jnp.where(lane < ROW, after, side)
        if b > 0:
            before = frame_ref[:, (b - 1) * TILE : b * TILE].astype(F32)
            side = jnp.where(lane >= TILE - ROW, before, side)
        out_ref[b, :, TILE:] = side.astype(BF)


def drive(step_ref, rows_ref, weight_ref, out_ref):
    blocks, channels, _ = rows_ref.shape
    states = weight_ref.shape[1]
    main = rows_ref[:, :, :TILE].reshape(blocks * channels, TILE)
    side = rows_ref[:, :, TILE:].reshape(blocks * channels, TILE)
    lane = lanes_of(main.shape)
    column = lanes_of((states, TILE)) % ROW
    total = None
    for i in range(3):
        if i == 0:
            source = jnp.where(lane >= TILE - ROW, side, main)
        elif i == 2:
            source = jnp.where(lane < ROW, side, main)
        else:
            source = main
        row = jnp.dot(weight_ref[3 * i + 1], source, preferred_element_type=F32)
        left = jnp.dot(weight_ref[3 * i], source, preferred_element_type=F32)
        right = jnp.dot(weight_ref[3 * i + 2], source, preferred_element_type=F32)
        row = row + jnp.where(column > 0, roll_lanes(left, 1), 0.0)
        row = row + jnp.where(column < ROW - 1, roll_lanes(right, -1), 0.0)
        row = roll_lanes(row, (1 - i) * ROW) if i != 1 else row
        total = row if total is None else total + row
    own = states // blocks
    rate = jnp.concatenate([collect(rows_ref[b, :own, TILE:], ROW) for b in range(blocks)], axis=0)
    decay = jnp.exp(-rate * step_ref[0])
    inject = jnp.sqrt(1.0 - decay * decay)
    scaled = (inject * total).astype(BF)
    meta = spread(decay, 0, (states, TILE)).astype(BF)
    group, part, _ = out_ref.shape
    for g in range(group):
        out_ref[g, :, :TILE] = scaled[g * part : (g + 1) * part]
        out_ref[g, :, TILE:] = meta[g * part : (g + 1) * part]


def finish_group(driven_ref, out_ref):
    frames, part, _ = driven_ref.shape
    state = None
    through = None
    for f in range(frames):
        decay = collect(driven_ref[f, :, TILE:], 0)
        value = driven_ref[f, :, :TILE].astype(F32)
        state = value if f == 0 else decay * state + value
        through = decay if f == 0 else decay * through
    final = state.astype(BF)
    meta = spread(through, 0, (part, TILE)).astype(BF)
    for g in range(out_ref.shape[0]):
        out_ref[g, :, :TILE] = final
        out_ref[g, :, TILE:] = meta


def run_group(at_ref, final_ref, driven_ref, out_ref):
    groups = final_ref.shape[0]
    frames, part, _ = driven_ref.shape
    at = at_ref[0]
    state = jnp.zeros((part, TILE), F32)
    for g in range(groups):
        through = collect(final_ref[g, :, TILE:], 0)
        moved = through * state + final_ref[g, :, :TILE].astype(F32)
        state = jnp.where(g < at, moved, state)
    copies = out_ref.shape[1]
    for f in range(frames):
        decay = collect(driven_ref[f, :, TILE:], 0)
        state = decay * state + driven_ref[f, :, :TILE].astype(F32)
        rounded = state.astype(BF)
        for c in range(copies):
            out_ref[f, c] = rounded


def finish(state_ref, frame_ref, weight_ref, gain_ref, out_ref):
    groups, blocks, part, _ = state_ref.shape
    states = groups * part
    channels, cells = frame_ref.shape
    tiles = [state_ref[:, b].reshape(states, TILE) for b in range(blocks)]
    lane = lanes_of((states, TILE))
    column = lanes_of((channels, cells)) % ROW
    total = None
    for i in range(3):
        if i == 1:
            source = jnp.concatenate(tiles, axis=1)
        else:
            parts = []
            for b in range(blocks):
                other = b + i - 1
                inside = 0 <= other < blocks
                beside = tiles[other] if inside else jnp.zeros_like(tiles[b])
                edge = lane < ROW if i == 2 else lane >= TILE - ROW
                parts.append(jnp.where(edge, beside, tiles[b]))
            source = jnp.concatenate(parts, axis=1)
        left = jnp.dot(weight_ref[3 * i], source, preferred_element_type=F32)
        row = jnp.dot(weight_ref[3 * i + 1], source, preferred_element_type=F32)
        right = jnp.dot(weight_ref[3 * i + 2], source, preferred_element_type=F32)
        row = row + jnp.where(column > 0, roll_lanes(left, 1), 0.0)
        row = row + jnp.where(column < ROW - 1, roll_lanes(right, -1), 0.0)
        if i != 1:
            row = jnp.concatenate(
                [
                    roll_lanes(row[:, b * TILE : (b + 1) * TILE], (1 - i) * ROW)
                    for b in range(blocks)
                ],
                axis=1,
            )
        total = row if total is None else total + row
    total = total + to_column(gain_ref[...]) * frame_ref[...].astype(F32)
    out_ref[...] = jax.nn.gelu(total).astype(BF)


def body(groups, frames, decay_rate, step_size, in_kernel, out_kernel, skip_gain):
    _, channels, cells = frames.shape
    blocks = cells // TILE
    states = in_kernel.shape[1]
    members = lax.axis_size("xc")
    part = states // members
    frame = frames.reshape(channels, cells)
    shape = jax.ShapeDtypeStruct
    cut = call(cut_rows, shape((blocks, channels, 2 * TILE), BF), frame, decay_rate[None])
    rows = lax.all_to_all(cut, "chan", 0, 0, tiled=True)
    driven = call(
        drive, shape((members, part, 2 * TILE), BF), step_size, rows, in_kernel, smem=(0,)
    )
    driven = lax.all_to_all(driven, "xc", 0, 0, tiled=True)
    final = call(finish_group, shape((groups, part, 2 * TILE), BF), driven)
    final = lax.all_to_all(final, "y", 0, 0, tiled=True)
    at = lax.axis_index("y").reshape(1)
    state = call(
        run_group, shape((members, blocks, part, TILE), BF), at, final, driven, smem=(0,)
    )
    state = state.reshape(members * blocks, part, TILE)
    state = lax.all_to_all(state, ("xc", "chan"), 0, 0, tiled=True)
    state = state.reshape(members, blocks, part, TILE)
    out = call(finish, shape((channels, cells), BF), state, frame, out_kernel, skip_gain[None])
    return out[None]


def solution(mesh):
    groups, members = 8, 8
    fine = Mesh(mesh.devices.reshape(groups, members, mesh.shape["chan"]), ("y", "xc", "chan"))
    time = ("y", "xc")
    in_specs = (P(time, "chan", None), P("chan"), P(time), P(), P(None, "chan", None), P("chan"))
    out_specs = P(time, "chan", None)
    return jax.shard_map(
        functools.partial(body, groups), mesh=fine, in_specs=in_specs, out_specs=out_specs, check_vma=False
    )
```

```python
import functools

import jax
import jax.numpy as jnp
from jax import lax
from jax.experimental import pallas as pl
from jax.experimental.pallas import tpu as pltpu
from jax.sharding import Mesh, PartitionSpec as P

ROW = 32
TILE = 128
BF = jnp.bfloat16
F32 = jnp.float32


def lanes_of(shape):
    return lax.broadcasted_iota(jnp.int32, shape, len(shape) - 1)


def roll_lanes(x, by):
    return pltpu.roll(x, by % x.shape[-1], len(x.shape) - 1)


def to_column(row):
    n = row.shape[-1]
    eye = lax.broadcasted_iota(jnp.int32, (n, n), 0) == lax.broadcasted_iota(jnp.int32, (n, n), 1)
    return jnp.sum(jnp.where(eye, jnp.broadcast_to(row, (n, n)), 0.0), axis=1, keepdims=True)


def pieces(column):
    high = column.astype(BF).astype(F32)
    rest = column - high
    mid = rest.astype(BF).astype(F32)
    return high, mid, rest - mid


def spread(column, at, shape):
    lane = lanes_of(shape)
    tile = jnp.zeros(shape, F32)
    for n, piece in enumerate(pieces(column)):
        tile = jnp.where(lane == at + n, piece, tile)
    return tile


def collect(tile, at):
    lane = lanes_of(tile.shape)
    inside = (lane >= at) & (lane < at + 3)
    return jnp.sum(jnp.where(inside, tile.astype(F32), 0.0), axis=-1, keepdims=True)


def call(kernel, outs, *operands, smem=(), vmem=32):
    specs = [
        pl.BlockSpec(memory_space=pltpu.SMEM if n in smem else pltpu.VMEM) for n in range(len(operands))
    ]
    return pl.pallas_call(
        kernel,
        out_shape=outs,
        in_specs=specs,
        out_specs=pl.BlockSpec(memory_space=pltpu.VMEM),
        compiler_params=pltpu.CompilerParams(vmem_limit_bytes=vmem << 20),
    )(*operands)


def cut_rows(frame_ref, rate_ref, out_ref):
    blocks = out_ref.shape[0]
    channels = out_ref.shape[1]
    lane = lanes_of((channels, TILE))
    own = to_column(rate_ref[...])
    column = jnp.concatenate([own, jnp.zeros((channels - own.shape[0], 1), F32)], axis=0)
    meta = spread(column, ROW, (channels, TILE))
    for b in range(blocks):
        out_ref[b, :, :TILE] = frame_ref[:, b * TILE : (b + 1) * TILE]
        side = meta
        if b + 1 < blocks:
            after = frame_ref[:, (b + 1) * TILE : (b + 2) * TILE].astype(F32)
            side = jnp.where(lane < ROW, after, side)
        if b > 0:
            before = frame_ref[:, (b - 1) * TILE : b * TILE].astype(F32)
            side = jnp.where(lane >= TILE - ROW, before, side)
        out_ref[b, :, TILE:] = side.astype(BF)


def drive(step_ref, rows_ref, weight_ref, out_ref):
    blocks, channels, _ = rows_ref.shape
    states = weight_ref.shape[1]
    main = rows_ref[:, :, :TILE].reshape(blocks * channels, TILE)
    side = rows_ref[:, :, TILE:].reshape(blocks * channels, TILE)
    lane = lanes_of(main.shape)
    column = lanes_of((states, TILE)) % ROW
    total = None
    for i in range(3):
        if i == 0:
            source = jnp.where(lane >= TILE - ROW, side, main)
        elif i == 2:
            source = jnp.where(lane < ROW, side, main)
        else:
            source = main
        row = jnp.dot(weight_ref[3 * i + 1], source, preferred_element_type=F32)
        left = jnp.dot(weight_ref[3 * i], source, preferred_element_type=F32)
        right = jnp.dot(weight_ref[3 * i + 2], source, preferred_element_type=F32)
        row = row + jnp.where(column > 0, roll_lanes(left, 1), 0.0)
        row = row + jnp.where(column < ROW - 1, roll_lanes(right, -1), 0.0)
        row = roll_lanes(row, (1 - i) * ROW) if i != 1 else row
        total = row if total is None else total + row
    own = states // blocks
    rate = jnp.concatenate([collect(rows_ref[b, :own, TILE:], ROW) for b in range(blocks)], axis=0)
    decay = jnp.exp(-rate * step_ref[0])
    inject = jnp.sqrt(1.0 - decay * decay)
    scaled = (inject * total).astype(BF)
    meta = spread(decay, 0, (states, TILE)).astype(BF)
    group, part, _ = out_ref.shape
    for g in range(group):
        out_ref[g, :, :TILE] = scaled[g * part : (g + 1) * part]
        out_ref[g, :, TILE:] = meta[g * part : (g + 1) * part]


def finish_group(driven_ref, out_ref):
    frames, part, _ = driven_ref.shape
    state = None
    through = None
    for f in range(frames):
        decay = collect(driven_ref[f, :, TILE:], 0)
        value = driven_ref[f, :, :TILE].astype(F32)
        state = value if f == 0 else decay * state + value
        through = decay if f == 0 else decay * through
    final = state.astype(BF)
    meta = spread(through, 0, (part, TILE)).astype(BF)
    for g in range(out_ref.shape[0]):
        out_ref[g, :, :TILE] = final
        out_ref[g, :, TILE:] = meta


def run_group(at_ref, final_ref, driven_ref, out_ref):
    groups = final_ref.shape[0]
    frames, part, _ = driven_ref.shape
    at = at_ref[0]
    state = jnp.zeros((part, TILE), F32)
    for g in range(groups):
        through = collect(final_ref[g, :, TILE:], 0)
        moved = through * state + final_ref[g, :, :TILE].astype(F32)
        state = jnp.where(g < at, moved, state)
    for f in range(frames):
        decay = collect(driven_ref[f, :, TILE:], 0)
        state = decay * state + driven_ref[f, :, :TILE].astype(F32)
        out_ref[f] = state.astype(BF)


def mix(state_ref, weight_ref, out_ref):
    groups, part, _ = state_ref.shape
    blocks, _, channels, states = weight_ref.shape
    source = state_ref[...].reshape(states, TILE)
    lane = lanes_of((blocks * channels, TILE))
    column = lane % ROW

    def weight(o):
        return weight_ref[:, o].reshape(blocks * channels, states)

    rows = []
    for i in range(3):
        left = jnp.dot(weight(3 * i), source, preferred_element_type=F32)
        row = jnp.dot(weight(3 * i + 1), source, preferred_element_type=F32)
        right = jnp.dot(weight(3 * i + 2), source, preferred_element_type=F32)
        row = row + jnp.where(column > 0, roll_lanes(left, 1), 0.0)
        row = row + jnp.where(column < ROW - 1, roll_lanes(right, -1), 0.0)
        rows.append(row)
    down = roll_lanes(rows[0], ROW)
    up = roll_lanes(rows[2], -ROW)
    main = rows[1] + jnp.where(lane >= ROW, down, 0.0) + jnp.where(lane < TILE - ROW, up, 0.0)
    side = jnp.where(lane < ROW, down, jnp.where(lane >= TILE - ROW, up, 0.0))
    out_ref[:, :, :TILE] = main.astype(BF).reshape(blocks, channels, TILE)
    out_ref[:, :, TILE:] = side.astype(BF).reshape(blocks, channels, TILE)


def finish(mixed_ref, frame_ref, gain_ref, out_ref):
    blocks, channels, _ = mixed_ref.shape
    lane = lanes_of((channels, TILE))
    gain = to_column(gain_ref[...])
    for b in range(blocks):
        at = slice(b * TILE, (b + 1) * TILE)
        total = mixed_ref[b, :, :TILE].astype(F32) + gain * frame_ref[:, at].astype(F32)
        if b > 0:
            total = total + jnp.where(lane < ROW, mixed_ref[b - 1, :, TILE:].astype(F32), 0.0)
        if b + 1 < blocks:
            total = total + jnp.where(lane >= TILE - ROW, mixed_ref[b + 1, :, TILE:].astype(F32), 0.0)
        out_ref[:, at] = jax.nn.gelu(total).astype(BF)


def body(groups, frames, decay_rate, step_size, in_kernel, out_kernel, skip_gain):
    _, channels, cells = frames.shape
    blocks = cells // TILE
    states = in_kernel.shape[1]
    members = lax.axis_size("xc")
    part = states // members
    frame = frames.reshape(channels, cells)
    shape = jax.ShapeDtypeStruct
    out_all = lax.all_gather(out_kernel, "chan", axis=0)
    cut = call(cut_rows, shape((blocks, channels, 2 * TILE), BF), frame, decay_rate[None])
    rows = lax.all_to_all(cut, "chan", 0, 0, tiled=True)
    driven = call(
        drive, shape((members, part, 2 * TILE), BF), step_size, rows, in_kernel, smem=(0,)
    )
    driven = lax.all_to_all(driven, "xc", 0, 0, tiled=True)
    final = call(finish_group, shape((groups, part, 2 * TILE), BF), driven)
    final = lax.all_to_all(final, "y", 0, 0, tiled=True)
    at = lax.axis_index("y").reshape(1)
    state = call(run_group, shape((members, part, TILE), BF), at, final, driven, smem=(0,))
    state = lax.all_to_all(state, "xc", 0, 0, tiled=True)
    mixed = call(mix, shape((blocks, channels, 2 * TILE), BF), state, out_all)
    mixed = lax.all_to_all(mixed, "chan", 0, 0, tiled=True)
    out = call(finish, shape((channels, cells), BF), mixed, frame, skip_gain[None])
    return out[None]


def solution(mesh):
    groups, members = 8, 8
    fine = Mesh(mesh.devices.reshape(groups, members, mesh.shape["chan"]), ("y", "xc", "chan"))
    time = ("y", "xc")
    in_specs = (P(time, "chan", None), P("chan"), P(time), P(), P(None, "chan", None), P("chan"))
    out_specs = P(time, "chan", None)
    return jax.shard_map(
        functools.partial(body, groups), mesh=fine, in_specs=in_specs, out_specs=out_specs, check_vma=False
    )
```

```python
import functools

import jax
import jax.numpy as jnp
from jax import lax
from jax.experimental import pallas as pl
from jax.experimental.pallas import tpu as pltpu
from jax.sharding import Mesh, PartitionSpec as P

ROW = 32
TILE = 128
BF = jnp.bfloat16
F32 = jnp.float32


def lanes_of(shape):
    return lax.broadcasted_iota(jnp.int32, shape, len(shape) - 1)


def roll_lanes(x, by):
    return pltpu.roll(x, by % x.shape[-1], len(x.shape) - 1)


def to_column(row):
    n = row.shape[-1]
    eye = lax.broadcasted_iota(jnp.int32, (n, n), 0) == lax.broadcasted_iota(jnp.int32, (n, n), 1)
    return jnp.sum(jnp.where(eye, jnp.broadcast_to(row, (n, n)), 0.0), axis=1, keepdims=True)


def pieces(column):
    high = column.astype(BF).astype(F32)
    rest = column - high
    mid = rest.astype(BF).astype(F32)
    return high, mid, rest - mid


def spread(column, at, shape):
    lane = lanes_of(shape)
    tile = jnp.zeros(shape, F32)
    for n, piece in enumerate(pieces(column)):
        tile = jnp.where(lane == at + n, piece, tile)
    return tile


def collect(tile, at):
    lane = lanes_of(tile.shape)
    inside = (lane >= at) & (lane < at + 3)
    return jnp.sum(jnp.where(inside, tile.astype(F32), 0.0), axis=-1, keepdims=True)


def call(kernel, outs, *operands, vmem=32):
    here = pl.BlockSpec(memory_space=pltpu.VMEM)
    return pl.pallas_call(
        kernel,
        out_shape=outs,
        in_specs=[here] * len(operands),
        out_specs=here,
        compiler_params=pltpu.CompilerParams(vmem_limit_bytes=vmem << 20),
    )(*operands)


def cut_rows(frame_ref, pace_ref, out_ref):
    blocks = out_ref.shape[0]
    channels = out_ref.shape[1]
    lane = lanes_of((channels, TILE))
    own = to_column(pace_ref[:, 1:])
    column = jnp.concatenate([own, jnp.zeros((channels - own.shape[0], 1), F32)], axis=0)
    meta = spread(column, ROW, (channels, TILE))
    for b in range(blocks):
        out_ref[b, :, :TILE] = frame_ref[:, b * TILE : (b + 1) * TILE]
        side = meta
        if b + 1 < blocks:
            after = frame_ref[:, (b + 1) * TILE : (b + 2) * TILE].astype(F32)
            side = jnp.where(lane < ROW, after, side)
        if b > 0:
            before = frame_ref[:, (b - 1) * TILE : b * TILE].astype(F32)
            side = jnp.where(lane >= TILE - ROW, before, side)
        out_ref[b, :, TILE:] = side.astype(BF)


def drive(pace_ref, rows_ref, weight_ref, out_ref):
    blocks, channels, _ = rows_ref.shape
    states = weight_ref.shape[1]
    main = rows_ref[:, :, :TILE].reshape(blocks * channels, TILE)
    side = rows_ref[:, :, TILE:].reshape(blocks * channels, TILE)
    lane = lanes_of(main.shape)
    column = lanes_of((states, TILE)) % ROW
    total = None
    for i in range(3):
        if i == 0:
            source = jnp.where(lane >= TILE - ROW, side, main)
        elif i == 2:
            source = jnp.where(lane < ROW, side, main)
        else:
            source = main
        row = jnp.dot(weight_ref[3 * i + 1], source, preferred_element_type=F32)
        left = jnp.dot(weight_ref[3 * i], source, preferred_element_type=F32)
        right = jnp.dot(weight_ref[3 * i + 2], source, preferred_element_type=F32)
        row = row + jnp.where(column > 0, roll_lanes(left, 1), 0.0)
        row = row + jnp.where(column < ROW - 1, roll_lanes(right, -1), 0.0)
        row = roll_lanes(row, (1 - i) * ROW) if i != 1 else row
        total = row if total is None else total + row
    own = states // blocks
    rate = jnp.concatenate([collect(rows_ref[b, :own, TILE:], ROW) for b in range(blocks)], axis=0)
    decay = jnp.exp(-rate * pace_ref[:, :1])
    inject = jnp.sqrt(1.0 - decay * decay)
    scaled = (inject * total).astype(BF)
    meta = spread(decay, 0, (states, TILE)).astype(BF)
    group, part, _ = out_ref.shape
    for g in range(group):
        out_ref[g, :, :TILE] = scaled[g * part : (g + 1) * part]
        out_ref[g, :, TILE:] = meta[g * part : (g + 1) * part]


def finish_group(driven_ref, out_ref):
    frames, part, _ = driven_ref.shape
    state = None
    through = None
    for f in range(frames):
        decay = collect(driven_ref[f, :, TILE:], 0)
        value = driven_ref[f, :, :TILE].astype(F32)
        state = value if f == 0 else decay * state + value
        through = decay if f == 0 else decay * through
    final = state.astype(BF)
    meta = spread(through, 0, (part, TILE)).astype(BF)
    for g in range(out_ref.shape[0]):
        out_ref[g, :, :TILE] = final
        out_ref[g, :, TILE:] = meta


def run_group(final_ref, driven_ref, out_ref):
    groups = final_ref.shape[0]
    frames, part, _ = driven_ref.shape
    at = lax.axis_index("y")
    state = jnp.zeros((part, TILE), F32)
    for g in range(groups):
        through = collect(final_ref[g, :, TILE:], 0)
        moved = through * state + final_ref[g, :, :TILE].astype(F32)
        state = jnp.where(g < at, moved, state)
    copies = out_ref.shape[1]
    for f in range(frames):
        decay = collect(driven_ref[f, :, TILE:], 0)
        state = decay * state + driven_ref[f, :, :TILE].astype(F32)
        rounded = state.astype(BF)
        for c in range(copies):
            out_ref[f, c] = rounded


def finish(state_ref, frame_ref, weight_ref, gain_ref, out_ref):
    groups, blocks, part, _ = state_ref.shape
    states = groups * part
    channels, cells = frame_ref.shape
    tiles = [state_ref[:, b].reshape(states, TILE) for b in range(blocks)]
    lane = lanes_of((states, TILE))
    column = lanes_of((channels, cells)) % ROW
    total = None
    for i in range(3):
        if i == 1:
            source = jnp.concatenate(tiles, axis=1)
        else:
            parts = []
            for b in range(blocks):
                other = b + i - 1
                inside = 0 <= other < blocks
                beside = tiles[other] if inside else jnp.zeros_like(tiles[b])
                edge = lane < ROW if i == 2 else lane >= TILE - ROW
                parts.append(jnp.where(edge, beside, tiles[b]))
            source = jnp.concatenate(parts, axis=1)
        left = jnp.dot(weight_ref[3 * i], source, preferred_element_type=F32)
        row = jnp.dot(weight_ref[3 * i + 1], source, preferred_element_type=F32)
        right = jnp.dot(weight_ref[3 * i + 2], source, preferred_element_type=F32)
        row = row + jnp.where(column > 0, roll_lanes(left, 1), 0.0)
        row = row + jnp.where(column < ROW - 1, roll_lanes(right, -1), 0.0)
        if i != 1:
            row = jnp.concatenate(
                [
                    roll_lanes(row[:, b * TILE : (b + 1) * TILE], (1 - i) * ROW)
                    for b in range(blocks)
                ],
                axis=1,
            )
        total = row if total is None else total + row
    total = total + to_column(gain_ref[...]) * frame_ref[...].astype(F32)
    out_ref[...] = jax.nn.gelu(total).astype(BF)


def body(groups, frames, decay_rate, step_size, in_kernel, out_kernel, skip_gain):
    _, channels, cells = frames.shape
    blocks = cells // TILE
    states = in_kernel.shape[1]
    members = lax.axis_size("xc")
    part = states // members
    frame = frames.reshape(channels, cells)
    shape = jax.ShapeDtypeStruct
    pace = jnp.concatenate([step_size, decay_rate])[None]
    cut = call(cut_rows, shape((blocks, channels, 2 * TILE), BF), frame, pace)
    rows = lax.all_to_all(cut, "chan", 0, 0, tiled=True)
    driven = call(drive, shape((members, part, 2 * TILE), BF), pace, rows, in_kernel)
    driven = lax.all_to_all(driven, "xc", 0, 0, tiled=True)
    final = call(finish_group, shape((groups, part, 2 * TILE), BF), driven)
    final = lax.all_to_all(final, "y", 0, 0, tiled=True)
    state = call(run_group, shape((members, blocks, part, TILE), BF), final, driven)
    state = state.reshape(members * blocks, part, TILE)
    state = lax.all_to_all(state, ("xc", "chan"), 0, 0, tiled=True)
    state = state.reshape(members, blocks, part, TILE)
    out = call(finish, shape((channels, cells), BF), state, frame, out_kernel, skip_gain[None])
    return out[None]


def solution(mesh):
    groups, members = 8, 8
    fine = Mesh(mesh.devices.reshape(groups, members, mesh.shape["chan"]), ("y", "xc", "chan"))
    time = ("y", "xc")
    in_specs = (P(time, "chan", None), P("chan"), P(time), P(), P(None, "chan", None), P("chan"))
    out_specs = P(time, "chan", None)
    return jax.shard_map(
        functools.partial(body, groups), mesh=fine, in_specs=in_specs, out_specs=out_specs, check_vma=False
    )
```

```python
import functools

import jax
import jax.numpy as jnp
from jax import lax
from jax.experimental import pallas as pl
from jax.experimental.pallas import tpu as pltpu
from jax.sharding import Mesh, PartitionSpec as P

ROW = 32
TILE = 128
BF = jnp.bfloat16
F32 = jnp.float32


def lanes_of(shape):
    return lax.broadcasted_iota(jnp.int32, shape, len(shape) - 1)


def roll_lanes(x, by):
    return pltpu.roll(x, by % x.shape[-1], len(x.shape) - 1)


def to_column(row):
    n = row.shape[-1]
    eye = lax.broadcasted_iota(jnp.int32, (n, n), 0) == lax.broadcasted_iota(jnp.int32, (n, n), 1)
    return jnp.sum(jnp.where(eye, jnp.broadcast_to(row, (n, n)), 0.0), axis=1, keepdims=True)


def pieces(column):
    high = column.astype(BF).astype(F32)
    rest = column - high
    mid = rest.astype(BF).astype(F32)
    return high, mid, rest - mid


def spread(column, at, shape):
    lane = lanes_of(shape)
    tile = jnp.zeros(shape, F32)
    for n, piece in enumerate(pieces(column)):
        tile = jnp.where(lane == at + n, piece, tile)
    return tile


def collect(tile, at):
    lane = lanes_of(tile.shape)
    inside = (lane >= at) & (lane < at + 3)
    return jnp.sum(jnp.where(inside, tile.astype(F32), 0.0), axis=-1, keepdims=True)


def call(kernel, outs, *operands, places=None, scratch=(), vmem=32, cost=None):
    places = places or (pltpu.VMEM,) * len(operands)
    specs = [pl.BlockSpec(memory_space=place) for place in places]
    return pl.pallas_call(
        kernel,
        out_shape=outs,
        in_specs=specs,
        out_specs=pl.BlockSpec(memory_space=pltpu.VMEM),
        scratch_shapes=scratch,
        cost_estimate=cost,
        compiler_params=pltpu.CompilerParams(vmem_limit_bytes=vmem << 20),
    )(*operands)


def cut_rows(frame_hbm, rate_hbm, out_ref, frame_ref, rate_ref, sems):
    copies = [
        pltpu.make_async_copy(source, target, sems.at[n])
        for n, (source, target) in enumerate([(frame_hbm, frame_ref), (rate_hbm, rate_ref)])
    ]
    for copy in copies:
        copy.start()
    for copy in copies:
        copy.wait()
    blocks = out_ref.shape[0]
    channels = frame_ref.shape[0]
    half = channels // 2
    lane = lanes_of((channels, TILE))
    after_at, before_at = lane < ROW, lane >= TILE - ROW
    near = lane[:half]
    outer = (near < ROW) | (near >= TILE - ROW)
    rate = to_column(rate_ref[...])
    part = rate.shape[0] // 2
    meta = spread(rate[:part], 0, (part, TILE)) + spread(rate[part:], 3, (part, TILE))
    meta = meta.astype(BF)
    for b in range(blocks):
        out_ref[b, :channels] = frame_ref[:, b * TILE : (b + 1) * TILE]
        side = jnp.zeros((channels, TILE), F32)
        if b + 1 < blocks:
            after = frame_ref[:, (b + 1) * TILE : (b + 2) * TILE].astype(F32)
            side = jnp.where(after_at, after, side)
        if b > 0:
            before = frame_ref[:, (b - 1) * TILE : b * TILE].astype(F32)
            side = jnp.where(before_at, before, side)
        packed = jnp.where(outer, side[:half], roll_lanes(side[half:], TILE // 2))
        out_ref[b, channels : channels + half] = packed.astype(BF)
        out_ref[b, channels + half :] = meta


def drive(step_ref, rows_ref, weight_ref, out_ref):
    blocks, height, _ = rows_ref.shape
    states, depth = weight_ref.shape[1:]
    channels = depth // blocks
    half = channels // 2
    main = rows_ref[:, :channels].reshape(depth, TILE)
    sides = []
    rates = []
    for b in range(blocks):
        packed = rows_ref[b, channels : channels + half]
        sides += [packed, roll_lanes(packed.astype(F32), TILE // 2).astype(BF)]
        meta = rows_ref[b, channels + half :]
        rates += [collect(meta, 0), collect(meta, 3)]
    side = jnp.concatenate(sides, axis=0)
    lane = lanes_of(main.shape)
    column = lanes_of((states, TILE)) % ROW
    total = None
    for i in range(3):
        if i == 0:
            source = jnp.where(lane >= TILE - ROW, side, main)
        elif i == 2:
            source = jnp.where(lane < ROW, side, main)
        else:
            source = main
        weight = weight_ref[3 * i : 3 * i + 3].reshape(3 * states, depth)
        left, row, right = jnp.split(jnp.dot(weight, source, preferred_element_type=F32), 3)
        row = row + jnp.where(column > 0, roll_lanes(left, 1), 0.0)
        row = row + jnp.where(column < ROW - 1, roll_lanes(right, -1), 0.0)
        row = roll_lanes(row, (1 - i) * ROW) if i != 1 else row
        total = row if total is None else total + row
    decay = jnp.exp(-jnp.concatenate(rates, axis=0) * step_ref[0])
    inject = jnp.sqrt(1.0 - decay * decay)
    scaled = (inject * total).astype(BF)
    meta = spread(decay, 0, (states, TILE)).astype(BF)
    group, part, _ = out_ref.shape
    for g in range(group):
        out_ref[g, :, :TILE] = scaled[g * part : (g + 1) * part]
        out_ref[g, :, TILE:] = meta[g * part : (g + 1) * part]


def finish_group(driven_ref, out_ref):
    frames, part, _ = driven_ref.shape
    state = None
    through = None
    for f in range(frames):
        decay = collect(driven_ref[f, :, TILE:], 0)
        value = driven_ref[f, :, :TILE].astype(F32)
        state = value if f == 0 else decay * state + value
        through = decay if f == 0 else decay * through
    final = state.astype(BF)
    meta = spread(through, 0, (part, TILE)).astype(BF)
    for g in range(out_ref.shape[0]):
        out_ref[g, :, :TILE] = final
        out_ref[g, :, TILE:] = meta


def run_group(final_ref, driven_ref, out_ref):
    groups = final_ref.shape[0]
    frames, part, _ = driven_ref.shape
    at = lax.axis_index("y")
    state = jnp.zeros((part, TILE), F32)
    for g in range(groups):
        through = collect(final_ref[g, :, TILE:], 0)
        moved = through * state + final_ref[g, :, :TILE].astype(F32)
        state = jnp.where(g < at, moved, state)
    copies = out_ref.shape[1]
    for f in range(frames):
        decay = collect(driven_ref[f, :, TILE:], 0)
        state = decay * state + driven_ref[f, :, :TILE].astype(F32)
        rounded = state.astype(BF)
        for c in range(copies):
            out_ref[f, c] = rounded


def finish(state_ref, frame_ref, weight_ref, gain_ref, out_ref):
    groups, blocks, part, _ = state_ref.shape
    states = groups * part
    channels = frame_ref.shape[0]
    source = jnp.concatenate([state_ref[:, b].reshape(states, TILE) for b in range(blocks)], axis=1)
    weight = weight_ref[...].reshape(9 * channels, states)
    taps = jnp.dot(weight, source, preferred_element_type=F32)
    lane = lanes_of((channels, TILE))
    column = lane % ROW
    gain = to_column(gain_ref[...])

    def row(i, b):
        def tap(j):
            at = (3 * i + j) * channels
            return taps[at : at + channels, b * TILE : (b + 1) * TILE]

        left = jnp.where(column > 0, roll_lanes(tap(0), 1), 0.0)
        right = jnp.where(column < ROW - 1, roll_lanes(tap(2), -1), 0.0)
        return tap(1) + left + right

    down = [roll_lanes(row(0, b), ROW) for b in range(blocks)]
    up = [roll_lanes(row(2, b), -ROW) for b in range(blocks)]
    for b in range(blocks):
        at = slice(b * TILE, (b + 1) * TILE)
        before = down[b - 1] if b > 0 else 0.0
        after = up[b + 1] if b + 1 < blocks else 0.0
        total = row(1, b) + gain * frame_ref[:, at].astype(F32)
        total = total + jnp.where(lane < ROW, before, down[b])
        total = total + jnp.where(lane >= TILE - ROW, after, up[b])
        out_ref[:, at] = jax.nn.gelu(total).astype(BF)


def body(groups, frames, decay_rate, step_size, in_kernel, out_kernel, skip_gain):
    _, channels, cells = frames.shape
    blocks = cells // TILE
    states = in_kernel.shape[1]
    members = lax.axis_size("xc")
    part = states // members
    frame = frames.reshape(channels, cells)
    shape = jax.ShapeDtypeStruct
    rates = decay_rate.shape[0]
    cut = call(
        cut_rows,
        shape((blocks, channels + channels // 2 + rates // 2, TILE), BF),
        frame,
        decay_rate[None],
        places=(pltpu.HBM, pltpu.HBM),
        scratch=(
            pltpu.VMEM(frame.shape, BF),
            pltpu.VMEM((1, rates), F32),
            pltpu.SemaphoreType.DMA((2,)),
        ),
        vmem=56,
        cost=pl.CostEstimate(flops=10**9, bytes_accessed=3 * 10**7, transcendentals=0),
    )
    rows = lax.all_to_all(cut, "chan", 0, 0, tiled=True)
    driven = call(
        drive,
        shape((members, part, 2 * TILE), BF),
        step_size,
        rows,
        in_kernel,
        places=(pltpu.SMEM, pltpu.VMEM, pltpu.VMEM),
    )
    driven = lax.all_to_all(driven, "xc", 0, 0, tiled=True)
    final = call(finish_group, shape((groups, part, 2 * TILE), BF), driven)
    final = lax.all_to_all(final, "y", 0, 0, tiled=True)
    state = call(run_group, shape((members, blocks, part, TILE), BF), final, driven)
    state = state.reshape(members * blocks, part, TILE)
    state = lax.all_to_all(state, ("xc", "chan"), 0, 0, tiled=True)
    state = state.reshape(members, blocks, part, TILE)
    out = call(finish, shape((channels, cells), BF), state, frame, out_kernel, skip_gain[None])
    return out[None]


def solution(mesh):
    groups, members = 8, 8
    fine = Mesh(mesh.devices.reshape(groups, members, mesh.shape["chan"]), ("y", "xc", "chan"))
    time = ("y", "xc")
    in_specs = (P(time, "chan", None), P("chan"), P(time), P(), P(None, "chan", None), P("chan"))
    out_specs = P(time, "chan", None)
    return jax.shard_map(
        functools.partial(body, groups), mesh=fine, in_specs=in_specs, out_specs=out_specs, check_vma=False
    )
```

```python
import functools

import jax
import jax.numpy as jnp
from jax import lax
from jax.experimental import pallas as pl
from jax.experimental.pallas import tpu as pltpu
from jax.sharding import Mesh, PartitionSpec as P

ROW = 32
TILE = 128
BF = jnp.bfloat16
F32 = jnp.float32


def lanes_of(shape):
    return lax.broadcasted_iota(jnp.int32, shape, len(shape) - 1)


def roll_lanes(x, by):
    return pltpu.roll(x, by % x.shape[-1], len(x.shape) - 1)


def to_column(row):
    n = row.shape[-1]
    eye = lax.broadcasted_iota(jnp.int32, (n, n), 0) == lax.broadcasted_iota(jnp.int32, (n, n), 1)
    return jnp.sum(jnp.where(eye, jnp.broadcast_to(row, (n, n)), 0.0), axis=1, keepdims=True)


def pieces(column):
    high = column.astype(BF).astype(F32)
    rest = column - high
    mid = rest.astype(BF).astype(F32)
    return high, mid, rest - mid


def spread(column, at, shape):
    lane = lanes_of(shape)
    tile = jnp.zeros(shape, F32)
    for n, piece in enumerate(pieces(column)):
        tile = jnp.where(lane == at + n, piece, tile)
    return tile


def collect(tile, at):
    lane = lanes_of(tile.shape)
    inside = (lane >= at) & (lane < at + 3)
    return jnp.sum(jnp.where(inside, tile.astype(F32), 0.0), axis=-1, keepdims=True)


def call(kernel, outs, *operands, places=None, scratch=(), vmem=32, cost=None):
    places = places or (pltpu.VMEM,) * len(operands)
    specs = [pl.BlockSpec(memory_space=place) for place in places]
    return pl.pallas_call(
        kernel,
        out_shape=outs,
        in_specs=specs,
        out_specs=pl.BlockSpec(memory_space=pltpu.VMEM),
        scratch_shapes=scratch,
        cost_estimate=cost,
        compiler_params=pltpu.CompilerParams(vmem_limit_bytes=vmem << 20),
    )(*operands)


def lay_step(step_ref, out_ref):
    out_ref[...] = jnp.full(out_ref.shape, step_ref[0], F32)


def cut_rows(step_ref, frame_ref, rate_ref, out_ref):
    blocks = out_ref.shape[0]
    channels = frame_ref.shape[0]
    half = channels // 2
    lane = lanes_of((channels, TILE))
    after_at, before_at = lane < ROW, lane >= TILE - ROW
    near = lane[:half]
    outer = (near < ROW) | (near >= TILE - ROW)
    rate = to_column(rate_ref[...])
    part = rate.shape[0] // 2
    tile = (part, TILE)
    meta = spread(rate[:part], 0, tile) + spread(rate[part:], 3, tile)
    meta = (meta + spread(jnp.broadcast_to(step_ref[:1, :1], (part, 1)), 6, tile)).astype(BF)
    for b in range(blocks):
        out_ref[b, :channels] = frame_ref[:, b * TILE : (b + 1) * TILE]
        side = jnp.zeros((channels, TILE), F32)
        if b + 1 < blocks:
            after = frame_ref[:, (b + 1) * TILE : (b + 2) * TILE].astype(F32)
            side = jnp.where(after_at, after, side)
        if b > 0:
            before = frame_ref[:, (b - 1) * TILE : b * TILE].astype(F32)
            side = jnp.where(before_at, before, side)
        packed = jnp.where(outer, side[:half], roll_lanes(side[half:], TILE // 2))
        out_ref[b, channels : channels + half] = packed.astype(BF)
        out_ref[b, channels + half :] = meta


def drive(rows_ref, weight_ref, out_ref):
    blocks, height, _ = rows_ref.shape
    states, depth = weight_ref.shape[1:]
    channels = depth // blocks
    half = channels // 2
    main = rows_ref[:, :channels].reshape(depth, TILE)
    sides = []
    rates = []
    for b in range(blocks):
        packed = rows_ref[b, channels : channels + half]
        sides += [packed, roll_lanes(packed.astype(F32), TILE // 2).astype(BF)]
        meta = rows_ref[b, channels + half :]
        rates += [collect(meta, 0), collect(meta, 3)]
    side = jnp.concatenate(sides, axis=0)
    step = collect(rows_ref[0, channels + half : channels + half + 8], 6)[:1]
    lane = lanes_of(main.shape)
    column = lanes_of((states, TILE)) % ROW
    total = None
    for i in range(3):
        if i == 0:
            source = jnp.where(lane >= TILE - ROW, side, main)
        elif i == 2:
            source = jnp.where(lane < ROW, side, main)
        else:
            source = main
        weight = weight_ref[3 * i : 3 * i + 3].reshape(3 * states, depth)
        left, row, right = jnp.split(jnp.dot(weight, source, preferred_element_type=F32), 3)
        row = row + jnp.where(column > 0, roll_lanes(left, 1), 0.0)
        row = row + jnp.where(column < ROW - 1, roll_lanes(right, -1), 0.0)
        row = roll_lanes(row, (1 - i) * ROW) if i != 1 else row
        total = row if total is None else total + row
    decay = jnp.exp(-jnp.concatenate(rates, axis=0) * step)
    inject = jnp.sqrt(1.0 - decay * decay)
    scaled = (inject * total).astype(BF)
    meta = spread(decay, 0, (states, TILE)).astype(BF)
    group, part, _ = out_ref.shape
    for g in range(group):
        out_ref[g, :, :TILE] = scaled[g * part : (g + 1) * part]
        out_ref[g, :, TILE:] = meta[g * part : (g + 1) * part]


def finish_group(driven_ref, out_ref):
    frames, part, _ = driven_ref.shape
    state = None
    through = None
    for f in range(frames):
        decay = collect(driven_ref[f, :, TILE:], 0)
        value = driven_ref[f, :, :TILE].astype(F32)
        state = value if f == 0 else decay * state + value
        through = decay if f == 0 else decay * through
    final = state.astype(BF)
    meta = spread(through, 0, (part, TILE)).astype(BF)
    for g in range(out_ref.shape[0]):
        out_ref[g, :, :TILE] = final
        out_ref[g, :, TILE:] = meta


def run_group(final_ref, driven_ref, out_ref):
    groups = final_ref.shape[0]
    frames, part, _ = driven_ref.shape
    at = lax.axis_index("y")
    state = jnp.zeros((part, TILE), F32)
    for g in range(groups):
        through = collect(final_ref[g, :, TILE:], 0)
        moved = through * state + final_ref[g, :, :TILE].astype(F32)
        state = jnp.where(g < at, moved, state)
    copies = out_ref.shape[1]
    for f in range(frames):
        decay = collect(driven_ref[f, :, TILE:], 0)
        state = decay * state + driven_ref[f, :, :TILE].astype(F32)
        rounded = state.astype(BF)
        for c in range(copies):
            out_ref[f, c] = rounded


def finish(state_ref, frame_ref, weight_ref, gain_ref, out_ref):
    groups, blocks, part, _ = state_ref.shape
    states = groups * part
    channels = frame_ref.shape[0]
    source = jnp.concatenate([state_ref[:, b].reshape(states, TILE) for b in range(blocks)], axis=1)
    weight = weight_ref[...].reshape(9 * channels, states)
    taps = jnp.dot(weight, source, preferred_element_type=F32)
    lane = lanes_of((channels, TILE))
    column = lane % ROW
    gain = to_column(gain_ref[...])

    def row(i, b):
        def tap(j):
            at = (3 * i + j) * channels
            return taps[at : at + channels, b * TILE : (b + 1) * TILE]

        left = jnp.where(column > 0, roll_lanes(tap(0), 1), 0.0)
        right = jnp.where(column < ROW - 1, roll_lanes(tap(2), -1), 0.0)
        return tap(1) + left + right

    down = [roll_lanes(row(0, b), ROW) for b in range(blocks)]
    up = [roll_lanes(row(2, b), -ROW) for b in range(blocks)]
    for b in range(blocks):
        at = slice(b * TILE, (b + 1) * TILE)
        before = down[b - 1] if b > 0 else 0.0
        after = up[b + 1] if b + 1 < blocks else 0.0
        total = row(1, b) + gain * frame_ref[:, at].astype(F32)
        total = total + jnp.where(lane < ROW, before, down[b])
        total = total + jnp.where(lane >= TILE - ROW, after, up[b])
        out_ref[:, at] = jax.nn.gelu(total).astype(BF)


def body(groups, frames, decay_rate, step_size, in_kernel, out_kernel, skip_gain):
    _, channels, cells = frames.shape
    blocks = cells // TILE
    states = in_kernel.shape[1]
    members = lax.axis_size("xc")
    part = states // members
    frame = frames.reshape(channels, cells)
    shape = jax.ShapeDtypeStruct
    rates = decay_rate.shape[0]
    step = call(
        lay_step,
        shape((8, TILE), F32),
        step_size,
        places=(pltpu.SMEM,),
        cost=pl.CostEstimate(flops=10**9, bytes_accessed=0, transcendentals=0),
    )
    cut = call(
        cut_rows,
        shape((blocks, channels + channels // 2 + rates // 2, TILE), BF),
        step,
        frame,
        decay_rate[None],
        cost=pl.CostEstimate(flops=10**9, bytes_accessed=0, transcendentals=0),
    )
    rows = lax.all_to_all(cut, "chan", 0, 0, tiled=True)
    driven = call(
        drive,
        shape((members, part, 2 * TILE), BF),
        rows,
        in_kernel,
    )
    driven = lax.all_to_all(driven, "xc", 0, 0, tiled=True)
    final = call(finish_group, shape((groups, part, 2 * TILE), BF), driven)
    final = lax.all_to_all(final, "y", 0, 0, tiled=True)
    state = call(run_group, shape((members, blocks, part, TILE), BF), final, driven)
    state = state.reshape(members * blocks, part, TILE)
    state = lax.all_to_all(state, ("xc", "chan"), 0, 0, tiled=True)
    state = state.reshape(members, blocks, part, TILE)
    out = call(finish, shape((channels, cells), BF), state, frame, out_kernel, skip_gain[None])
    return out[None]


def solution(mesh):
    groups, members = 8, 8
    fine = Mesh(mesh.devices.reshape(groups, members, mesh.shape["chan"]), ("y", "xc", "chan"))
    time = ("y", "xc")
    in_specs = (P(time, "chan", None), P("chan"), P(time), P(), P(None, "chan", None), P("chan"))
    out_specs = P(time, "chan", None)
    return jax.shard_map(
        functools.partial(body, groups), mesh=fine, in_specs=in_specs, out_specs=out_specs, check_vma=False
    )
```

```python
import functools

import jax
import jax.numpy as jnp
from jax import lax
from jax.experimental import pallas as pl
from jax.experimental.pallas import tpu as pltpu
from jax.sharding import Mesh, PartitionSpec as P

ROW = 32
TILE = 128
BF = jnp.bfloat16
F32 = jnp.float32


def lanes_of(shape):
    return lax.broadcasted_iota(jnp.int32, shape, len(shape) - 1)


def roll_lanes(x, by):
    return pltpu.roll(x, by % x.shape[-1], len(x.shape) - 1)


def to_column(row):
    n = row.shape[-1]
    eye = lax.broadcasted_iota(jnp.int32, (n, n), 0) == lax.broadcasted_iota(jnp.int32, (n, n), 1)
    return jnp.sum(jnp.where(eye, jnp.broadcast_to(row, (n, n)), 0.0), axis=1, keepdims=True)


def pieces(column):
    high = column.astype(BF).astype(F32)
    rest = column - high
    mid = rest.astype(BF).astype(F32)
    return high, mid, rest - mid


def spread(column, at, shape):
    lane = lanes_of(shape)
    tile = jnp.zeros(shape, F32)
    for n, piece in enumerate(pieces(column)):
        tile = jnp.where(lane == at + n, piece, tile)
    return tile


def collect(tile, at):
    lane = lanes_of(tile.shape)
    inside = (lane >= at) & (lane < at + 3)
    return jnp.sum(jnp.where(inside, tile.astype(F32), 0.0), axis=-1, keepdims=True)


def call(kernel, outs, *operands, places=None, scratch=(), vmem=32, cost=None):
    places = places or (pltpu.VMEM,) * len(operands)
    specs = [pl.BlockSpec(memory_space=place) for place in places]
    return pl.pallas_call(
        kernel,
        out_shape=outs,
        in_specs=specs,
        out_specs=pl.BlockSpec(memory_space=pltpu.VMEM),
        scratch_shapes=scratch,
        cost_estimate=cost,
        compiler_params=pltpu.CompilerParams(vmem_limit_bytes=vmem << 20),
    )(*operands)


def lay_step(step_ref, out_ref):
    out_ref[...] = jnp.full(out_ref.shape, step_ref[0], F32)


def cut_rows(order, step_ref, frame_ref, rate_ref, out_ref):
    blocks = out_ref.shape[0]
    channels = frame_ref.shape[0]
    half = channels // 2
    lane = lanes_of((channels, TILE))
    after_at, before_at = lane < ROW, lane >= TILE - ROW
    near = lane[:half]
    outer = (near < ROW) | (near >= TILE - ROW)
    rate = to_column(rate_ref[...])
    part = rate.shape[0] // 2
    tile = (part, TILE)
    meta = spread(rate[:part], 0, tile) + spread(rate[part:], 3, tile)
    meta = (meta + spread(jnp.broadcast_to(step_ref[:1, :1], (part, 1)), 6, tile)).astype(BF)
    for at, b in enumerate(order):
        out_ref[at, :channels] = frame_ref[:, b * TILE : (b + 1) * TILE]
        side = jnp.zeros((channels, TILE), F32)
        if b + 1 < blocks:
            after = frame_ref[:, (b + 1) * TILE : (b + 2) * TILE].astype(F32)
            side = jnp.where(after_at, after, side)
        if b > 0:
            before = frame_ref[:, (b - 1) * TILE : b * TILE].astype(F32)
            side = jnp.where(before_at, before, side)
        packed = jnp.where(outer, side[:half], roll_lanes(side[half:], TILE // 2))
        out_ref[at, channels : channels + half] = packed.astype(BF)
        out_ref[at, channels + half :] = meta


def drive(order, part_order, rows_ref, weight_ref, out_ref):
    blocks, height, _ = rows_ref.shape
    states, depth = weight_ref.shape[1:]
    channels = depth // blocks
    half = channels // 2
    main = jnp.concatenate([rows_ref[order.index(b), :channels] for b in range(blocks)], axis=0)
    sides = []
    rates = []
    for b in range(blocks):
        at = order.index(b)
        packed = rows_ref[at, channels : channels + half]
        sides += [packed, roll_lanes(packed.astype(F32), TILE // 2).astype(BF)]
        meta = rows_ref[at, channels + half :]
        rates += [collect(meta, 0), collect(meta, 3)]
    side = jnp.concatenate(sides, axis=0)
    step = collect(rows_ref[0, channels + half : channels + half + 8], 6)[:1]
    lane = lanes_of(main.shape)
    column = lanes_of((states, TILE)) % ROW
    total = None
    for i in range(3):
        if i == 0:
            source = jnp.where(lane >= TILE - ROW, side, main)
        elif i == 2:
            source = jnp.where(lane < ROW, side, main)
        else:
            source = main
        weight = weight_ref[3 * i : 3 * i + 3].reshape(3 * states, depth)
        left, row, right = jnp.split(jnp.dot(weight, source, preferred_element_type=F32), 3)
        row = row + jnp.where(column > 0, roll_lanes(left, 1), 0.0)
        row = row + jnp.where(column < ROW - 1, roll_lanes(right, -1), 0.0)
        row = roll_lanes(row, (1 - i) * ROW) if i != 1 else row
        total = row if total is None else total + row
    decay = jnp.exp(-jnp.concatenate(rates, axis=0) * step)
    inject = jnp.sqrt(1.0 - decay * decay)
    scaled = (inject * total).astype(BF)
    meta = spread(decay, 0, (states, TILE)).astype(BF)
    group, part, _ = out_ref.shape
    for at, g in enumerate(part_order):
        out_ref[at, :, :TILE] = scaled[g * part : (g + 1) * part]
        out_ref[at, :, TILE:] = meta[g * part : (g + 1) * part]


def finish_group(order, driven_ref, out_ref):
    frames, part, _ = driven_ref.shape
    state = None
    through = None
    for f in range(frames):
        at = order.index(f)
        decay = collect(driven_ref[at, :, TILE:], 0)
        value = driven_ref[at, :, :TILE].astype(F32)
        state = value if f == 0 else decay * state + value
        through = decay if f == 0 else decay * through
    final = state.astype(BF)
    meta = spread(through, 0, (part, TILE)).astype(BF)
    for g in range(out_ref.shape[0]):
        out_ref[g, :, :TILE] = final
        out_ref[g, :, TILE:] = meta


def run_group(order, frame_order, spread_order, final_ref, driven_ref, out_ref):
    groups = final_ref.shape[0]
    frames, part, _ = driven_ref.shape
    at = lax.axis_index("y")
    state = jnp.zeros((part, TILE), F32)
    for g in range(groups):
        source = order.index(g)
        through = collect(final_ref[source, :, TILE:], 0)
        moved = through * state + final_ref[source, :, :TILE].astype(F32)
        state = jnp.where(g < at, moved, state)
    copies = out_ref.shape[0] // frames
    for f in range(frames):
        source = frame_order.index(f)
        decay = collect(driven_ref[source, :, TILE:], 0)
        state = decay * state + driven_ref[source, :, :TILE].astype(F32)
        rounded = state.astype(BF)
        for c in range(copies):
            out_ref[spread_order.index(f * copies + c)] = rounded


def finish(order, state_ref, frame_ref, weight_ref, gain_ref, out_ref):
    channels, cells = frame_ref.shape
    blocks = cells // TILE
    states = weight_ref.shape[2]
    parts = len(order) // blocks

    def rows(b):
        return jnp.concatenate([state_ref[order.index(p * blocks + b)] for p in range(parts)], axis=0)

    source = jnp.concatenate([rows(b) for b in range(blocks)], axis=1)
    weight = weight_ref[...].reshape(9 * channels, states)
    taps = jnp.dot(weight, source, preferred_element_type=F32)
    lane = lanes_of((channels, TILE))
    column = lane % ROW
    gain = to_column(gain_ref[...])

    def row(i, b):
        def tap(j):
            at = (3 * i + j) * channels
            return taps[at : at + channels, b * TILE : (b + 1) * TILE]

        left = jnp.where(column > 0, roll_lanes(tap(0), 1), 0.0)
        right = jnp.where(column < ROW - 1, roll_lanes(tap(2), -1), 0.0)
        return tap(1) + left + right

    down = [roll_lanes(row(0, b), ROW) for b in range(blocks)]
    up = [roll_lanes(row(2, b), -ROW) for b in range(blocks)]
    for b in range(blocks):
        at = slice(b * TILE, (b + 1) * TILE)
        before = down[b - 1] if b > 0 else 0.0
        after = up[b + 1] if b + 1 < blocks else 0.0
        total = row(1, b) + gain * frame_ref[:, at].astype(F32)
        total = total + jnp.where(lane < ROW, before, down[b])
        total = total + jnp.where(lane >= TILE - ROW, after, up[b])
        out_ref[:, at] = jax.nn.gelu(total).astype(BF)


Z_ORDER = [0, 4, 2, 6, 1, 5, 3, 7]
Y_ORDER = [0, 4, 2, 6, 1, 5, 3, 7]
X_ORDER = [0, 1, 2, 3, 4, 5, 6, 7]
S_ORDER = [i * 8 + k for i in [0, 2, 4, 6, 1, 3, 5, 7] for k in Z_ORDER]


def exchange(x, axis, order):
    return lax.all_to_all(x, axis, 0, 0, axis_index_groups=[order], tiled=True)


def body(groups, frames, decay_rate, step_size, in_kernel, out_kernel, skip_gain):
    _, channels, cells = frames.shape
    blocks = cells // TILE
    states = in_kernel.shape[1]
    members = lax.axis_size("xc")
    part = states // members
    frame = frames.reshape(channels, cells)
    shape = jax.ShapeDtypeStruct
    rates = decay_rate.shape[0]
    step = call(
        lay_step,
        shape((8, TILE), F32),
        step_size,
        places=(pltpu.SMEM,),
        cost=pl.CostEstimate(flops=10**9, bytes_accessed=0, transcendentals=0),
    )
    cut = call(
        functools.partial(cut_rows, Z_ORDER),
        shape((blocks, channels + channels // 2 + rates // 2, TILE), BF),
        step,
        frame,
        decay_rate[None],
        cost=pl.CostEstimate(flops=10**9, bytes_accessed=0, transcendentals=0),
    )
    rows = exchange(cut, "chan", Z_ORDER)
    driven = call(
        functools.partial(drive, Z_ORDER, X_ORDER),
        shape((members, part, 2 * TILE), BF),
        rows,
        in_kernel,
    )
    driven = exchange(driven, "xc", X_ORDER)
    final = call(functools.partial(finish_group, X_ORDER), shape((groups, part, 2 * TILE), BF), driven)
    final = exchange(final, "y", Y_ORDER)
    state = call(
        functools.partial(run_group, Y_ORDER, X_ORDER, S_ORDER),
        shape((members * blocks, part, TILE), BF),
        final,
        driven,
    )
    state = exchange(state, ("xc", "chan"), S_ORDER)
    out = call(
        functools.partial(finish, S_ORDER),
        shape((channels, cells), BF),
        state,
        frame,
        out_kernel,
        skip_gain[None],
    )
    return out[None]


def solution(mesh):
    groups, members = 8, 8
    fine = Mesh(mesh.devices.reshape(groups, members, mesh.shape["chan"]), ("y", "xc", "chan"))
    time = ("y", "xc")
    in_specs = (P(time, "chan", None), P("chan"), P(time), P(), P(None, "chan", None), P("chan"))
    out_specs = P(time, "chan", None)
    return jax.shard_map(
        functools.partial(body, groups), mesh=fine, in_specs=in_specs, out_specs=out_specs, check_vma=False
    )
```

```python
import functools

import jax
import jax.numpy as jnp
from jax import lax
from jax.experimental import pallas as pl
from jax.experimental.pallas import tpu as pltpu
from jax.sharding import Mesh, PartitionSpec as P

ROW = 32
TILE = 128
BF = jnp.bfloat16
F32 = jnp.float32


def lanes_of(shape):
    return lax.broadcasted_iota(jnp.int32, shape, len(shape) - 1)


def roll_lanes(x, by):
    return pltpu.roll(x, by % x.shape[-1], len(x.shape) - 1)


def to_column(row):
    n = row.shape[-1]
    eye = lax.broadcasted_iota(jnp.int32, (n, n), 0) == lax.broadcasted_iota(jnp.int32, (n, n), 1)
    return jnp.sum(jnp.where(eye, jnp.broadcast_to(row, (n, n)), 0.0), axis=1, keepdims=True)


def pieces(column):
    high = column.astype(BF).astype(F32)
    rest = column - high
    mid = rest.astype(BF).astype(F32)
    return high, mid, rest - mid


def spread(column, at, shape):
    lane = lanes_of(shape)
    tile = jnp.zeros(shape, F32)
    for n, piece in enumerate(pieces(column)):
        tile = jnp.where(lane == at + n, piece, tile)
    return tile


def collect(tile, at):
    lane = lanes_of(tile.shape)
    inside = (lane >= at) & (lane < at + 3)
    return jnp.sum(jnp.where(inside, tile.astype(F32), 0.0), axis=-1, keepdims=True)


def call(kernel, outs, *operands, places=None, scratch=(), vmem=32, cost=None):
    places = places or (pltpu.VMEM,) * len(operands)
    specs = [pl.BlockSpec(memory_space=place) for place in places]
    return pl.pallas_call(
        kernel,
        out_shape=outs,
        in_specs=specs,
        out_specs=pl.BlockSpec(memory_space=pltpu.VMEM),
        scratch_shapes=scratch,
        cost_estimate=cost,
        compiler_params=pltpu.CompilerParams(vmem_limit_bytes=vmem << 20),
    )(*operands)


def lay_step(step_ref, out_ref):
    out_ref[...] = jnp.full(out_ref.shape, step_ref[0], F32)


def cut_rows(order, step_ref, frame_ref, rate_ref, out_ref):
    blocks = out_ref.shape[0]
    channels = frame_ref.shape[0]
    half = channels // 2
    lane = lanes_of((channels, TILE))
    after_at, before_at = lane < ROW, lane >= TILE - ROW
    near = lane[:half]
    outer = (near < ROW) | (near >= TILE - ROW)
    rate = to_column(rate_ref[...])
    part = rate.shape[0] // 2
    tile = (part, TILE)
    meta = spread(rate[:part], 0, tile) + spread(rate[part:], 3, tile)
    meta = (meta + spread(jnp.broadcast_to(step_ref[:1, :1], (part, 1)), 6, tile)).astype(BF)
    for at, b in enumerate(order):
        out_ref[at, :channels] = frame_ref[:, b * TILE : (b + 1) * TILE]
        side = jnp.zeros((channels, TILE), F32)
        if b + 1 < blocks:
            after = frame_ref[:, (b + 1) * TILE : (b + 2) * TILE].astype(F32)
            side = jnp.where(after_at, after, side)
        if b > 0:
            before = frame_ref[:, (b - 1) * TILE : b * TILE].astype(F32)
            side = jnp.where(before_at, before, side)
        packed = jnp.where(outer, side[:half], roll_lanes(side[half:], TILE // 2))
        out_ref[at, channels : channels + half] = packed.astype(BF)
        out_ref[at, channels + half :] = meta


def drive(order, part_order, rows_ref, weight_ref, out_ref):
    blocks, height, _ = rows_ref.shape
    states, depth = weight_ref.shape[1:]
    channels = depth // blocks
    half = channels // 2
    main = jnp.concatenate([rows_ref[order.index(b), :channels] for b in range(blocks)], axis=0)
    sides = []
    rates = []
    for b in range(blocks):
        at = order.index(b)
        packed = rows_ref[at, channels : channels + half]
        sides += [packed, roll_lanes(packed.astype(F32), TILE // 2).astype(BF)]
        meta = rows_ref[at, channels + half :]
        rates += [collect(meta, 0), collect(meta, 3)]
    side = jnp.concatenate(sides, axis=0)
    step = collect(rows_ref[0, channels + half : channels + half + 8], 6)[:1]
    lane = lanes_of(main.shape)
    column = lanes_of((states, TILE)) % ROW
    total = None
    for i in range(3):
        if i == 0:
            source = jnp.where(lane >= TILE - ROW, side, main)
        elif i == 2:
            source = jnp.where(lane < ROW, side, main)
        else:
            source = main
        weight = weight_ref[3 * i : 3 * i + 3].reshape(3 * states, depth)
        left, row, right = jnp.split(jnp.dot(weight, source, preferred_element_type=F32), 3)
        row = row + jnp.where(column > 0, roll_lanes(left, 1), 0.0)
        row = row + jnp.where(column < ROW - 1, roll_lanes(right, -1), 0.0)
        row = roll_lanes(row, (1 - i) * ROW) if i != 1 else row
        total = row if total is None else total + row
    decay = jnp.exp(-jnp.concatenate(rates, axis=0) * step)
    inject = jnp.sqrt(1.0 - decay * decay)
    scaled = (inject * total).astype(BF)
    meta = spread(decay, 0, (states, TILE)).astype(BF)
    group, part, _ = out_ref.shape
    for at, g in enumerate(part_order):
        out_ref[at, :, :TILE] = scaled[g * part : (g + 1) * part]
        out_ref[at, :, TILE:] = meta[g * part : (g + 1) * part]


def finish_group(order, driven_ref, out_ref):
    frames, part, _ = driven_ref.shape
    state = None
    through = None
    for f in range(frames):
        at = order.index(f)
        decay = collect(driven_ref[at, :, TILE:], 0)
        value = driven_ref[at, :, :TILE].astype(F32)
        state = value if f == 0 else decay * state + value
        through = decay if f == 0 else decay * through
    final = state.astype(BF)
    meta = spread(through, 0, (part, TILE)).astype(BF)
    for g in range(out_ref.shape[0]):
        out_ref[g, :, :TILE] = final
        out_ref[g, :, TILE:] = meta


def run_group(order, frame_order, spread_order, final_ref, driven_ref, out_ref):
    groups = final_ref.shape[0]
    frames, part, _ = driven_ref.shape
    at = lax.axis_index("y")
    state = jnp.zeros((part, TILE), F32)
    for g in range(groups):
        source = order.index(g)
        through = collect(final_ref[source, :, TILE:], 0)
        moved = through * state + final_ref[source, :, :TILE].astype(F32)
        state = jnp.where(g < at, moved, state)
    copies = out_ref.shape[0] // frames
    for f in range(frames):
        source = frame_order.index(f)
        decay = collect(driven_ref[source, :, TILE:], 0)
        state = decay * state + driven_ref[source, :, :TILE].astype(F32)
        rounded = state.astype(BF)
        for c in range(copies):
            out_ref[spread_order.index(f * copies + c)] = rounded


def finish(order, state_ref, frame_ref, weight_ref, gain_ref, out_ref):
    channels, cells = frame_ref.shape
    blocks = cells // TILE
    states = weight_ref.shape[2]
    parts = len(order) // blocks

    def rows(b):
        return jnp.concatenate([state_ref[order.index(p * blocks + b)] for p in range(parts)], axis=0)

    source = jnp.concatenate([rows(b) for b in range(blocks)], axis=1)
    weight = weight_ref[...].reshape(9 * channels, states)
    taps = jnp.dot(weight, source, preferred_element_type=F32)
    lane = lanes_of((channels, TILE))
    column = lane % ROW
    gain = to_column(gain_ref[...])

    def row(i, b):
        def tap(j):
            at = (3 * i + j) * channels
            return taps[at : at + channels, b * TILE : (b + 1) * TILE]

        left = jnp.where(column > 0, roll_lanes(tap(0), 1), 0.0)
        right = jnp.where(column < ROW - 1, roll_lanes(tap(2), -1), 0.0)
        return tap(1) + left + right

    down = [roll_lanes(row(0, b), ROW) for b in range(blocks)]
    up = [roll_lanes(row(2, b), -ROW) for b in range(blocks)]
    for b in range(blocks):
        at = slice(b * TILE, (b + 1) * TILE)
        before = down[b - 1] if b > 0 else 0.0
        after = up[b + 1] if b + 1 < blocks else 0.0
        total = row(1, b) + gain * frame_ref[:, at].astype(F32)
        total = total + jnp.where(lane < ROW, before, down[b])
        total = total + jnp.where(lane >= TILE - ROW, after, up[b])
        out_ref[:, at] = jax.nn.gelu(total).astype(BF)


Z_ORDER = [5, 1, 7, 3, 4, 2, 6, 0]
Y_ORDER = [4, 0, 6, 2, 5, 1, 7, 3]
X_ORDER = [5, 4, 7, 6, 1, 0, 3, 2]
S_ORDER = [i * 8 + k for i in [5, 7, 0, 2, 4, 6, 1, 3] for k in [4, 2, 6, 1, 5, 3, 7, 0]]


def exchange(x, axis, order):
    return lax.all_to_all(x, axis, 0, 0, axis_index_groups=[order], tiled=True)


def body(groups, frames, decay_rate, step_size, in_kernel, out_kernel, skip_gain):
    _, channels, cells = frames.shape
    blocks = cells // TILE
    states = in_kernel.shape[1]
    members = lax.axis_size("xc")
    part = states // members
    frame = frames.reshape(channels, cells)
    shape = jax.ShapeDtypeStruct
    rates = decay_rate.shape[0]
    step = call(
        lay_step,
        shape((8, TILE), F32),
        step_size,
        places=(pltpu.SMEM,),
        cost=pl.CostEstimate(flops=10**9, bytes_accessed=0, transcendentals=0),
    )
    cut = call(
        functools.partial(cut_rows, Z_ORDER),
        shape((blocks, channels + channels // 2 + rates // 2, TILE), BF),
        step,
        frame,
        decay_rate[None],
        cost=pl.CostEstimate(flops=10**9, bytes_accessed=0, transcendentals=0),
    )
    rows = exchange(cut, "chan", Z_ORDER)
    driven = call(
        functools.partial(drive, Z_ORDER, X_ORDER),
        shape((members, part, 2 * TILE), BF),
        rows,
        in_kernel,
    )
    driven = exchange(driven, "xc", X_ORDER)
    final = call(functools.partial(finish_group, X_ORDER), shape((groups, part, 2 * TILE), BF), driven)
    final = exchange(final, "y", Y_ORDER)
    state = call(
        functools.partial(run_group, Y_ORDER, X_ORDER, S_ORDER),
        shape((members * blocks, part, TILE), BF),
        final,
        driven,
    )
    state = exchange(state, ("xc", "chan"), S_ORDER)
    out = call(
        functools.partial(finish, S_ORDER),
        shape((channels, cells), BF),
        state,
        frame,
        out_kernel,
        skip_gain[None],
    )
    return out[None]


def solution(mesh):
    groups, members = 8, 8
    fine = Mesh(mesh.devices.reshape(groups, members, mesh.shape["chan"]), ("y", "xc", "chan"))
    time = ("y", "xc")
    in_specs = (P(time, "chan", None), P("chan"), P(time), P(), P(None, "chan", None), P("chan"))
    out_specs = P(time, "chan", None)
    return jax.shard_map(
        functools.partial(body, groups), mesh=fine, in_specs=in_specs, out_specs=out_specs, check_vma=False
    )
```

```python
import functools

import jax
import jax.numpy as jnp
from jax import lax
from jax.experimental import pallas as pl
from jax.experimental.pallas import tpu as pltpu
from jax.sharding import Mesh, PartitionSpec as P

ROW = 32
TILE = 128
BF = jnp.bfloat16
F32 = jnp.float32


def lanes_of(shape):
    return lax.broadcasted_iota(jnp.int32, shape, len(shape) - 1)


def roll_lanes(x, by):
    return pltpu.roll(x, by % x.shape[-1], len(x.shape) - 1)


def to_column(row):
    n = row.shape[-1]
    eye = lax.broadcasted_iota(jnp.int32, (n, n), 0) == lax.broadcasted_iota(jnp.int32, (n, n), 1)
    return jnp.sum(jnp.where(eye, jnp.broadcast_to(row, (n, n)), 0.0), axis=1, keepdims=True)


def pieces(column):
    high = column.astype(BF).astype(F32)
    rest = column - high
    mid = rest.astype(BF).astype(F32)
    return high, mid, rest - mid


def spread(column, at, shape):
    lane = lanes_of(shape)
    tile = jnp.zeros(shape, F32)
    for n, piece in enumerate(pieces(column)):
        tile = jnp.where(lane == at + n, piece, tile)
    return tile


def collect(tile, at):
    lane = lanes_of(tile.shape)
    inside = (lane >= at) & (lane < at + 3)
    return jnp.sum(jnp.where(inside, tile.astype(F32), 0.0), axis=-1, keepdims=True)


def call(kernel, outs, *operands, places=None, scratch=(), vmem=32, cost=None):
    places = places or (pltpu.VMEM,) * len(operands)
    specs = [pl.BlockSpec(memory_space=place) for place in places]
    return pl.pallas_call(
        kernel,
        out_shape=outs,
        in_specs=specs,
        out_specs=pl.BlockSpec(memory_space=pltpu.VMEM),
        scratch_shapes=scratch,
        cost_estimate=cost,
        compiler_params=pltpu.CompilerParams(vmem_limit_bytes=vmem << 20),
    )(*operands)


def lay_step(step_ref, out_ref):
    out_ref[...] = jnp.full(out_ref.shape, step_ref[0], F32)


def cut_rows(order, step_ref, frame_ref, rate_ref, out_ref):
    blocks = out_ref.shape[0]
    channels = frame_ref.shape[0]
    half = channels // 2
    lane = lanes_of((channels, TILE))
    after_at, before_at = lane < ROW, lane >= TILE - ROW
    near = lane[:half]
    outer = (near < ROW) | (near >= TILE - ROW)
    rate = to_column(rate_ref[...])
    part = rate.shape[0] // 2
    tile = (part, TILE)
    meta = spread(rate[:part], 0, tile) + spread(rate[part:], 3, tile)
    meta = (meta + spread(jnp.broadcast_to(step_ref[:1, :1], (part, 1)), 6, tile)).astype(BF)
    for at, b in enumerate(order):
        out_ref[at, :channels] = frame_ref[:, b * TILE : (b + 1) * TILE]
        side = jnp.zeros((channels, TILE), F32)
        if b + 1 < blocks:
            after = frame_ref[:, (b + 1) * TILE : (b + 2) * TILE].astype(F32)
            side = jnp.where(after_at, after, side)
        if b > 0:
            before = frame_ref[:, (b - 1) * TILE : b * TILE].astype(F32)
            side = jnp.where(before_at, before, side)
        packed = jnp.where(outer, side[:half], roll_lanes(side[half:], TILE // 2))
        out_ref[at, channels : channels + half] = packed.astype(BF)
        out_ref[at, channels + half :] = meta


def drive(order, part_order, rows_ref, weight_ref, out_ref):
    blocks, height, _ = rows_ref.shape
    states, depth = weight_ref.shape[1:]
    channels = depth // blocks
    half = channels // 2
    main = jnp.concatenate([rows_ref[order.index(b), :channels] for b in range(blocks)], axis=0)
    sides = []
    rates = []
    for b in range(blocks):
        at = order.index(b)
        packed = rows_ref[at, channels : channels + half]
        sides += [packed, roll_lanes(packed.astype(F32), TILE // 2).astype(BF)]
        meta = rows_ref[at, channels + half :]
        rates += [collect(meta, 0), collect(meta, 3)]
    side = jnp.concatenate(sides, axis=0)
    step = collect(rows_ref[0, channels + half : channels + half + 8], 6)[:1]
    lane = lanes_of(main.shape)
    column = lanes_of((states, TILE)) % ROW
    total = None
    for i in range(3):
        if i == 0:
            source = jnp.where(lane >= TILE - ROW, side, main)
        elif i == 2:
            source = jnp.where(lane < ROW, side, main)
        else:
            source = main
        weight = weight_ref[3 * i : 3 * i + 3].reshape(3 * states, depth)
        left, row, right = jnp.split(jnp.dot(weight, source, preferred_element_type=F32), 3)
        row = row + jnp.where(column > 0, roll_lanes(left, 1), 0.0)
        row = row + jnp.where(column < ROW - 1, roll_lanes(right, -1), 0.0)
        row = roll_lanes(row, (1 - i) * ROW) if i != 1 else row
        total = row if total is None else total + row
    decay = jnp.exp(-jnp.concatenate(rates, axis=0) * step)
    inject = jnp.sqrt(1.0 - decay * decay)
    scaled = (inject * total).astype(BF)
    meta = spread(decay, 0, (states, TILE)).astype(BF)
    group, part, _ = out_ref.shape
    for at, g in enumerate(part_order):
        out_ref[at, :, :TILE] = scaled[g * part : (g + 1) * part]
        out_ref[at, :, TILE:] = meta[g * part : (g + 1) * part]


def finish_group(order, driven_ref, out_ref):
    frames, part, _ = driven_ref.shape
    state = None
    through = None
    for f in range(frames):
        at = order.index(f)
        decay = collect(driven_ref[at, :, TILE:], 0)
        value = driven_ref[at, :, :TILE].astype(F32)
        state = value if f == 0 else decay * state + value
        through = decay if f == 0 else decay * through
    final = state.astype(BF)
    meta = spread(through, 0, (part, TILE)).astype(BF)
    for g in range(out_ref.shape[0]):
        out_ref[g, :, :TILE] = final
        out_ref[g, :, TILE:] = meta


def run_group(order, frame_order, spread_order, final_ref, driven_ref, out_ref):
    groups = final_ref.shape[0]
    frames, part, _ = driven_ref.shape
    at = lax.axis_index("y")
    state = jnp.zeros((part, TILE), F32)
    for g in range(groups):
        source = order.index(g)
        through = collect(final_ref[source, :, TILE:], 0)
        moved = through * state + final_ref[source, :, :TILE].astype(F32)
        state = jnp.where(g < at, moved, state)
    copies = out_ref.shape[0] // frames
    for f in range(frames):
        source = frame_order.index(f)
        decay = collect(driven_ref[source, :, TILE:], 0)
        state = decay * state + driven_ref[source, :, :TILE].astype(F32)
        rounded = state.astype(BF)
        for c in range(copies):
            out_ref[spread_order.index(f * copies + c)] = rounded


def finish(order, state_ref, frame_ref, weight_ref, gain_ref, out_ref):
    channels, cells = frame_ref.shape
    blocks = cells // TILE
    states = weight_ref.shape[2]
    parts = len(order) // blocks

    def rows(b):
        return jnp.concatenate([state_ref[order.index(p * blocks + b)] for p in range(parts)], axis=0)

    source = jnp.concatenate([rows(b) for b in range(blocks)], axis=1)
    weight = weight_ref[...].reshape(9 * channels, states)
    taps = jnp.dot(weight, source, preferred_element_type=F32)
    lane = lanes_of((channels, TILE))
    column = lane % ROW
    gain = to_column(gain_ref[...])

    def row(i, b):
        def tap(j):
            at = (3 * i + j) * channels
            return taps[at : at + channels, b * TILE : (b + 1) * TILE]

        left = jnp.where(column > 0, roll_lanes(tap(0), 1), 0.0)
        right = jnp.where(column < ROW - 1, roll_lanes(tap(2), -1), 0.0)
        return tap(1) + left + right

    down = [roll_lanes(row(0, b), ROW) for b in range(blocks)]
    up = [roll_lanes(row(2, b), -ROW) for b in range(blocks)]
    for b in range(blocks):
        at = slice(b * TILE, (b + 1) * TILE)
        before = down[b - 1] if b > 0 else 0.0
        after = up[b + 1] if b + 1 < blocks else 0.0
        total = row(1, b) + gain * frame_ref[:, at].astype(F32)
        total = total + jnp.where(lane < ROW, before, down[b])
        total = total + jnp.where(lane >= TILE - ROW, after, up[b])
        out_ref[:, at] = jax.nn.gelu(total).astype(BF)


Z_ORDER = [5, 1, 7, 3, 4, 2, 6, 0]
Y_ORDER = [4, 2, 6, 1, 5, 3, 7, 0]
X_ORDER = [5, 7, 1, 3, 4, 6, 0, 2]
S_ORDER = [i * 8 + k for ks in ([4, 6, 5, 3, 7], [2, 1, 0]) for i in [5, 7, 0, 2, 4, 6, 1, 3] for k in ks]


def exchange(x, axis, order):
    return lax.all_to_all(x, axis, 0, 0, axis_index_groups=[order], tiled=True)


def body(groups, frames, decay_rate, step_size, in_kernel, out_kernel, skip_gain):
    _, channels, cells = frames.shape
    blocks = cells // TILE
    states = in_kernel.shape[1]
    members = lax.axis_size("xc")
    part = states // members
    frame = frames.reshape(channels, cells)
    shape = jax.ShapeDtypeStruct
    rates = decay_rate.shape[0]
    step = call(
        lay_step,
        shape((8, TILE), F32),
        step_size,
        places=(pltpu.SMEM,),
        cost=pl.CostEstimate(flops=10**9, bytes_accessed=0, transcendentals=0),
    )
    cut = call(
        functools.partial(cut_rows, Z_ORDER),
        shape((blocks, channels + channels // 2 + rates // 2, TILE), BF),
        step,
        frame,
        decay_rate[None],
        cost=pl.CostEstimate(flops=10**9, bytes_accessed=0, transcendentals=0),
    )
    rows = exchange(cut, "chan", Z_ORDER)
    driven = call(
        functools.partial(drive, Z_ORDER, X_ORDER),
        shape((members, part, 2 * TILE), BF),
        rows,
        in_kernel,
    )
    driven = exchange(driven, "xc", X_ORDER)
    final = call(functools.partial(finish_group, X_ORDER), shape((groups, part, 2 * TILE), BF), driven)
    final = exchange(final, "y", Y_ORDER)
    state = call(
        functools.partial(run_group, Y_ORDER, X_ORDER, S_ORDER),
        shape((members * blocks, part, TILE), BF),
        final,
        driven,
    )
    state = exchange(state, ("xc", "chan"), S_ORDER)
    out = call(
        functools.partial(finish, S_ORDER),
        shape((channels, cells), BF),
        state,
        frame,
        out_kernel,
        skip_gain[None],
    )
    return out[None]


def solution(mesh):
    groups, members = 8, 8
    fine = Mesh(mesh.devices.reshape(groups, members, mesh.shape["chan"]), ("y", "xc", "chan"))
    time = ("y", "xc")
    in_specs = (P(time, "chan", None), P("chan"), P(time), P(), P(None, "chan", None), P("chan"))
    out_specs = P(time, "chan", None)
    return jax.shard_map(
        functools.partial(body, groups), mesh=fine, in_specs=in_specs, out_specs=out_specs, check_vma=False
    )
```

```python
import functools

import jax
import jax.numpy as jnp
from jax import lax
from jax.experimental import pallas as pl
from jax.experimental.pallas import tpu as pltpu
from jax.sharding import Mesh, PartitionSpec as P

ROW = 32
TILE = 128
BF = jnp.bfloat16
F32 = jnp.float32


def lanes_of(shape):
    return lax.broadcasted_iota(jnp.int32, shape, len(shape) - 1)


def roll_lanes(x, by):
    return pltpu.roll(x, by % x.shape[-1], len(x.shape) - 1)


def to_column(row):
    n = row.shape[-1]
    eye = lax.broadcasted_iota(jnp.int32, (n, n), 0) == lax.broadcasted_iota(jnp.int32, (n, n), 1)
    return jnp.sum(jnp.where(eye, jnp.broadcast_to(row, (n, n)), 0.0), axis=1, keepdims=True)


def pieces(column):
    high = column.astype(BF).astype(F32)
    rest = column - high
    mid = rest.astype(BF).astype(F32)
    return high, mid, rest - mid


def spread(column, at, shape):
    lane = lanes_of(shape)
    tile = jnp.zeros(shape, F32)
    for n, piece in enumerate(pieces(column)):
        tile = jnp.where(lane == at + n, piece, tile)
    return tile


def collect(tile, at):
    lane = lanes_of(tile.shape)
    inside = (lane >= at) & (lane < at + 3)
    return jnp.sum(jnp.where(inside, tile.astype(F32), 0.0), axis=-1, keepdims=True)


def diagonal(n):
    return lax.broadcasted_iota(jnp.int32, (n, TILE), 0) == lanes_of((n, TILE))


def lay_rows(column):
    n = column.shape[0]
    at = lax.broadcasted_iota(jnp.int32, (16, TILE), 0)
    tile = jnp.zeros((16, TILE), F32)
    for r, piece in enumerate(pieces(column)):
        row = jnp.sum(jnp.where(diagonal(n), piece, 0.0), axis=0, keepdims=True)
        tile = jnp.where(at == r, row, tile)
    return tile.astype(BF)


def read_rows(tile, n):
    row = jnp.sum(tile.astype(F32), axis=0, keepdims=True)
    return jnp.sum(jnp.where(diagonal(n), row, 0.0), axis=1, keepdims=True)


def call(kernel, outs, *operands, places=None, scratch=(), vmem=32, cost=None):
    places = places or (pltpu.VMEM,) * len(operands)
    specs = [pl.BlockSpec(memory_space=place) for place in places]
    return pl.pallas_call(
        kernel,
        out_shape=outs,
        in_specs=specs,
        out_specs=pl.BlockSpec(memory_space=pltpu.VMEM),
        scratch_shapes=scratch,
        cost_estimate=cost,
        compiler_params=pltpu.CompilerParams(vmem_limit_bytes=vmem << 20),
    )(*operands)


def lay_step(step_ref, out_ref):
    out_ref[...] = jnp.full(out_ref.shape, step_ref[0], F32)


def cut_rows(order, step_ref, frame_ref, rate_ref, out_ref):
    blocks = out_ref.shape[0]
    channels = frame_ref.shape[0]
    half = channels // 2
    lane = lanes_of((channels, TILE))
    after_at, before_at = lane < ROW, lane >= TILE - ROW
    near = lane[:half]
    outer = (near < ROW) | (near >= TILE - ROW)
    rate = to_column(rate_ref[...])
    part = rate.shape[0] // 2
    tile = (part, TILE)
    meta = spread(rate[:part], 0, tile) + spread(rate[part:], 3, tile)
    meta = (meta + spread(jnp.broadcast_to(step_ref[:1, :1], (part, 1)), 6, tile)).astype(BF)
    for at, b in enumerate(order):
        out_ref[at, :channels] = frame_ref[:, b * TILE : (b + 1) * TILE]
        side = jnp.zeros((channels, TILE), F32)
        if b + 1 < blocks:
            after = frame_ref[:, (b + 1) * TILE : (b + 2) * TILE].astype(F32)
            side = jnp.where(after_at, after, side)
        if b > 0:
            before = frame_ref[:, (b - 1) * TILE : b * TILE].astype(F32)
            side = jnp.where(before_at, before, side)
        packed = jnp.where(outer, side[:half], roll_lanes(side[half:], TILE // 2))
        out_ref[at, channels : channels + half] = packed.astype(BF)
        out_ref[at, channels + half :] = meta


def drive(order, part_order, rows_ref, weight_ref, out_ref):
    blocks, height, _ = rows_ref.shape
    states, depth = weight_ref.shape[1:]
    channels = depth // blocks
    half = channels // 2
    main = jnp.concatenate([rows_ref[order.index(b), :channels] for b in range(blocks)], axis=0)
    sides = []
    rates = []
    for b in range(blocks):
        at = order.index(b)
        packed = rows_ref[at, channels : channels + half]
        sides += [packed, roll_lanes(packed.astype(F32), TILE // 2).astype(BF)]
        meta = rows_ref[at, channels + half :]
        rates += [collect(meta, 0), collect(meta, 3)]
    side = jnp.concatenate(sides, axis=0)
    step = collect(rows_ref[0, channels + half : channels + half + 8], 6)[:1]
    lane = lanes_of(main.shape)
    column = lanes_of((states, TILE)) % ROW
    total = None
    for i in range(3):
        if i == 0:
            source = jnp.where(lane >= TILE - ROW, side, main)
        elif i == 2:
            source = jnp.where(lane < ROW, side, main)
        else:
            source = main
        weight = weight_ref[3 * i : 3 * i + 3].reshape(3 * states, depth)
        left, row, right = jnp.split(jnp.dot(weight, source, preferred_element_type=F32), 3)
        row = row + jnp.where(column > 0, roll_lanes(left, 1), 0.0)
        row = row + jnp.where(column < ROW - 1, roll_lanes(right, -1), 0.0)
        row = roll_lanes(row, (1 - i) * ROW) if i != 1 else row
        total = row if total is None else total + row
    decay = jnp.exp(-jnp.concatenate(rates, axis=0) * step)
    inject = jnp.sqrt(1.0 - decay * decay)
    scaled = (inject * total).astype(BF)
    part = states // len(part_order)
    for at, g in enumerate(part_order):
        out_ref[at, :part] = scaled[g * part : (g + 1) * part]
        out_ref[at, part:] = lay_rows(decay[g * part : (g + 1) * part])


def finish_group(order, driven_ref, out_ref):
    frames, height, _ = driven_ref.shape
    part = height - 16
    state = None
    through = None
    for f in range(frames):
        at = order.index(f)
        decay = read_rows(driven_ref[at, part:], part)
        value = driven_ref[at, :part].astype(F32)
        state = value if f == 0 else decay * state + value
        through = decay if f == 0 else decay * through
    final = state.astype(BF)
    meta = lay_rows(through)
    for g in range(out_ref.shape[0]):
        out_ref[g, :part] = final
        out_ref[g, part:] = meta


def run_group(order, frame_order, spread_order, final_ref, driven_ref, out_ref):
    groups = final_ref.shape[0]
    frames, height, _ = driven_ref.shape
    part = height - 16
    at = lax.axis_index("y")
    state = jnp.zeros((part, TILE), F32)
    for g in range(groups):
        source = order.index(g)
        through = read_rows(final_ref[source, part:], part)
        moved = through * state + final_ref[source, :part].astype(F32)
        state = jnp.where(g < at, moved, state)
    copies = out_ref.shape[0] // frames
    for f in range(frames):
        source = frame_order.index(f)
        decay = read_rows(driven_ref[source, part:], part)
        state = decay * state + driven_ref[source, :part].astype(F32)
        rounded = state.astype(BF)
        for c in range(copies):
            out_ref[spread_order.index(f * copies + c)] = rounded


def finish(order, state_ref, frame_ref, weight_ref, gain_ref, out_ref):
    channels, cells = frame_ref.shape
    blocks = cells // TILE
    states = weight_ref.shape[2]
    parts = len(order) // blocks

    def rows(b):
        return jnp.concatenate([state_ref[order.index(p * blocks + b)] for p in range(parts)], axis=0)

    source = jnp.concatenate([rows(b) for b in range(blocks)], axis=1)
    weight = weight_ref[...].reshape(9 * channels, states)
    taps = jnp.dot(weight, source, preferred_element_type=F32)
    lane = lanes_of((channels, TILE))
    column = lane % ROW
    gain = to_column(gain_ref[...])

    def row(i, b):
        def tap(j):
            at = (3 * i + j) * channels
            return taps[at : at + channels, b * TILE : (b + 1) * TILE]

        left = jnp.where(column > 0, roll_lanes(tap(0), 1), 0.0)
        right = jnp.where(column < ROW - 1, roll_lanes(tap(2), -1), 0.0)
        return tap(1) + left + right

    down = [roll_lanes(row(0, b), ROW) for b in range(blocks)]
    up = [roll_lanes(row(2, b), -ROW) for b in range(blocks)]
    for b in range(blocks):
        at = slice(b * TILE, (b + 1) * TILE)
        before = down[b - 1] if b > 0 else 0.0
        after = up[b + 1] if b + 1 < blocks else 0.0
        total = row(1, b) + gain * frame_ref[:, at].astype(F32)
        total = total + jnp.where(lane < ROW, before, down[b])
        total = total + jnp.where(lane >= TILE - ROW, after, up[b])
        out_ref[:, at] = jax.nn.gelu(total).astype(BF)


Z_ORDER = [5, 1, 7, 3, 4, 2, 6, 0]
Y_ORDER = [4, 2, 6, 1, 5, 3, 7, 0]
X_ORDER = [5, 7, 1, 3, 4, 6, 0, 2]
S_ORDER = [i * 8 + k for ks in ([4, 6, 5, 3, 7], [2, 1, 0]) for i in [5, 7, 0, 2, 4, 6, 1, 3] for k in ks]


def exchange(x, axis, order):
    return lax.all_to_all(x, axis, 0, 0, axis_index_groups=[order], tiled=True)


def body(groups, frames, decay_rate, step_size, in_kernel, out_kernel, skip_gain):
    _, channels, cells = frames.shape
    blocks = cells // TILE
    states = in_kernel.shape[1]
    members = lax.axis_size("xc")
    part = states // members
    frame = frames.reshape(channels, cells)
    shape = jax.ShapeDtypeStruct
    rates = decay_rate.shape[0]
    step = call(
        lay_step,
        shape((8, TILE), F32),
        step_size,
        places=(pltpu.SMEM,),
        cost=pl.CostEstimate(flops=10**9, bytes_accessed=0, transcendentals=0),
    )
    cut = call(
        functools.partial(cut_rows, Z_ORDER),
        shape((blocks, channels + channels // 2 + rates // 2, TILE), BF),
        step,
        frame,
        decay_rate[None],
        cost=pl.CostEstimate(flops=10**9, bytes_accessed=0, transcendentals=0),
    )
    rows = exchange(cut, "chan", Z_ORDER)
    driven = call(
        functools.partial(drive, Z_ORDER, X_ORDER),
        shape((members, part + 16, TILE), BF),
        rows,
        in_kernel,
    )
    driven = exchange(driven, "xc", X_ORDER)
    final = call(functools.partial(finish_group, X_ORDER), shape((groups, part + 16, TILE), BF), driven)
    final = exchange(final, "y", Y_ORDER)
    state = call(
        functools.partial(run_group, Y_ORDER, X_ORDER, S_ORDER),
        shape((members * blocks, part, TILE), BF),
        final,
        driven,
    )
    state = exchange(state, ("xc", "chan"), S_ORDER)
    out = call(
        functools.partial(finish, S_ORDER),
        shape((channels, cells), BF),
        state,
        frame,
        out_kernel,
        skip_gain[None],
    )
    return out[None]


def solution(mesh):
    groups, members = 8, 8
    fine = Mesh(mesh.devices.reshape(groups, members, mesh.shape["chan"]), ("y", "xc", "chan"))
    time = ("y", "xc")
    in_specs = (P(time, "chan", None), P("chan"), P(time), P(), P(None, "chan", None), P("chan"))
    out_specs = P(time, "chan", None)
    return jax.shard_map(
        functools.partial(body, groups), mesh=fine, in_specs=in_specs, out_specs=out_specs, check_vma=False
    )
```

```python
import functools

import jax
import jax.numpy as jnp
from jax import lax
from jax.experimental import pallas as pl
from jax.experimental.pallas import tpu as pltpu
from jax.sharding import Mesh, PartitionSpec as P

ROW = 32
TILE = 128
BF = jnp.bfloat16
F32 = jnp.float32


def lanes_of(shape):
    return lax.broadcasted_iota(jnp.int32, shape, len(shape) - 1)


def roll_lanes(x, by):
    return pltpu.roll(x, by % x.shape[-1], len(x.shape) - 1)


def to_column(row):
    n = row.shape[-1]
    eye = lax.broadcasted_iota(jnp.int32, (n, n), 0) == lax.broadcasted_iota(jnp.int32, (n, n), 1)
    return jnp.sum(jnp.where(eye, jnp.broadcast_to(row, (n, n)), 0.0), axis=1, keepdims=True)


def pieces(column):
    high = column.astype(BF).astype(F32)
    rest = column - high
    mid = rest.astype(BF).astype(F32)
    return high, mid, rest - mid


def spread(column, at, shape):
    lane = lanes_of(shape)
    tile = jnp.zeros(shape, F32)
    for n, piece in enumerate(pieces(column)):
        tile = jnp.where(lane == at + n, piece, tile)
    return tile


def collect(tile, at):
    lane = lanes_of(tile.shape)
    inside = (lane >= at) & (lane < at + 3)
    return jnp.sum(jnp.where(inside, tile.astype(F32), 0.0), axis=-1, keepdims=True)


def diagonal(n):
    return lax.broadcasted_iota(jnp.int32, (n, TILE), 0) == lanes_of((n, TILE))


def lay_rows(column):
    n = column.shape[0]
    at = lax.broadcasted_iota(jnp.int32, (8, TILE), 0)
    tile = jnp.zeros((8, TILE), F32)
    for r, piece in enumerate(pieces(column)):
        row = jnp.sum(jnp.where(diagonal(n), piece, 0.0), axis=0, keepdims=True)
        tile = jnp.where(at == r, row, tile)
    return tile.astype(BF)


def read_rows(tile, n):
    row = jnp.sum(tile.astype(F32), axis=0, keepdims=True)
    return jnp.sum(jnp.where(diagonal(n), row, 0.0), axis=1, keepdims=True)


def call(kernel, outs, *operands, places=None, scratch=(), vmem=32, cost=None):
    places = places or (pltpu.VMEM,) * len(operands)
    specs = [pl.BlockSpec(memory_space=place) for place in places]
    return pl.pallas_call(
        kernel,
        out_shape=outs,
        in_specs=specs,
        out_specs=pl.BlockSpec(memory_space=pltpu.VMEM),
        scratch_shapes=scratch,
        cost_estimate=cost,
        compiler_params=pltpu.CompilerParams(vmem_limit_bytes=vmem << 20),
    )(*operands)


def lay_step(step_ref, out_ref):
    out_ref[...] = jnp.full(out_ref.shape, step_ref[0], F32)


def cut_rows(order, step_ref, frame_ref, rate_ref, out_ref):
    blocks = out_ref.shape[0]
    channels = frame_ref.shape[0]
    half = channels // 2
    lane = lanes_of((channels, TILE))
    after_at, before_at = lane < ROW, lane >= TILE - ROW
    near = lane[:half]
    outer = (near < ROW) | (near >= TILE - ROW)
    rate = to_column(rate_ref[...])
    at = lax.broadcasted_iota(jnp.int32, (8, TILE), 0)
    meta = lay_rows(rate).astype(F32)
    for r, piece in enumerate(pieces(step_ref[:1])):
        meta = jnp.where(at == r + 3, piece, meta)
    meta = meta.astype(BF)
    for at, b in enumerate(order):
        out_ref[at, :channels] = frame_ref[:, b * TILE : (b + 1) * TILE]
        side = jnp.zeros((channels, TILE), F32)
        if b + 1 < blocks:
            after = frame_ref[:, (b + 1) * TILE : (b + 2) * TILE].astype(F32)
            side = jnp.where(after_at, after, side)
        if b > 0:
            before = frame_ref[:, (b - 1) * TILE : b * TILE].astype(F32)
            side = jnp.where(before_at, before, side)
        packed = jnp.where(outer, side[:half], roll_lanes(side[half:], TILE // 2))
        out_ref[at, channels : channels + half] = packed.astype(BF)
        out_ref[at, channels + half :] = meta


def drive(order, part_order, rows_ref, weight_ref, out_ref):
    blocks, height, _ = rows_ref.shape
    states, depth = weight_ref.shape[1:]
    channels = depth // blocks
    half = channels // 2
    main = jnp.concatenate([rows_ref[order.index(b), :channels] for b in range(blocks)], axis=0)
    sides = []
    rates = []
    for b in range(blocks):
        at = order.index(b)
        packed = rows_ref[at, channels : channels + half]
        sides += [packed, roll_lanes(packed.astype(F32), TILE // 2).astype(BF)]
        meta = rows_ref[at, channels + half :]
        rates.append(read_rows(meta[:3], states // blocks))
    side = jnp.concatenate(sides, axis=0)
    step = jnp.sum(rows_ref[0, channels + half + 3 : channels + half + 6].astype(F32), axis=0, keepdims=True)[:, :1]
    lane = lanes_of(main.shape)
    column = lanes_of((states, TILE)) % ROW
    total = None
    for i in range(3):
        if i == 0:
            source = jnp.where(lane >= TILE - ROW, side, main)
        elif i == 2:
            source = jnp.where(lane < ROW, side, main)
        else:
            source = main
        weight = weight_ref[3 * i : 3 * i + 3].reshape(3 * states, depth)
        left, row, right = jnp.split(jnp.dot(weight, source, preferred_element_type=F32), 3)
        row = row + jnp.where(column > 0, roll_lanes(left, 1), 0.0)
        row = row + jnp.where(column < ROW - 1, roll_lanes(right, -1), 0.0)
        row = roll_lanes(row, (1 - i) * ROW) if i != 1 else row
        total = row if total is None else total + row
    decay = jnp.exp(-jnp.concatenate(rates, axis=0) * step)
    inject = jnp.sqrt(1.0 - decay * decay)
    scaled = (inject * total).astype(BF)
    part = states // len(part_order)
    for at, g in enumerate(part_order):
        out_ref[at, :part] = scaled[g * part : (g + 1) * part]
        out_ref[at, part:] = lay_rows(decay[g * part : (g + 1) * part])


def finish_group(order, driven_ref, out_ref):
    frames, height, _ = driven_ref.shape
    part = height - 8
    state = None
    through = None
    for f in range(frames):
        at = order.index(f)
        decay = read_rows(driven_ref[at, part:], part)
        value = driven_ref[at, :part].astype(F32)
        state = value if f == 0 else decay * state + value
        through = decay if f == 0 else decay * through
    final = state.astype(BF)
    meta = lay_rows(through)
    for g in range(out_ref.shape[0]):
        out_ref[g, :part] = final
        out_ref[g, part:] = meta


def run_group(order, frame_order, spread_order, final_ref, driven_ref, out_ref):
    groups = final_ref.shape[0]
    frames, height, _ = driven_ref.shape
    part = height - 8
    at = lax.axis_index("y")
    state = jnp.zeros((part, TILE), F32)
    for g in range(groups):
        source = order.index(g)
        through = read_rows(final_ref[source, part:], part)
        moved = through * state + final_ref[source, :part].astype(F32)
        state = jnp.where(g < at, moved, state)
    copies = out_ref.shape[0] // frames
    for f in range(frames):
        source = frame_order.index(f)
        decay = read_rows(driven_ref[source, part:], part)
        state = decay * state + driven_ref[source, :part].astype(F32)
        rounded = state.astype(BF)
        for c in range(copies):
            out_ref[spread_order.index(f * copies + c)] = rounded


def finish(order, state_ref, frame_ref, weight_ref, gain_ref, out_ref):
    channels, cells = frame_ref.shape
    blocks = cells // TILE
    states = weight_ref.shape[2]
    parts = len(order) // blocks

    def rows(b):
        return jnp.concatenate([state_ref[order.index(p * blocks + b)] for p in range(parts)], axis=0)

    source = jnp.concatenate([rows(b) for b in range(blocks)], axis=1)
    weight = weight_ref[...].reshape(9 * channels, states)
    taps = jnp.dot(weight, source, preferred_element_type=F32)
    lane = lanes_of((channels, TILE))
    column = lane % ROW
    gain = to_column(gain_ref[...])

    def row(i, b):
        def tap(j):
            at = (3 * i + j) * channels
            return taps[at : at + channels, b * TILE : (b + 1) * TILE]

        left = jnp.where(column > 0, roll_lanes(tap(0), 1), 0.0)
        right = jnp.where(column < ROW - 1, roll_lanes(tap(2), -1), 0.0)
        return tap(1) + left + right

    down = [roll_lanes(row(0, b), ROW) for b in range(blocks)]
    up = [roll_lanes(row(2, b), -ROW) for b in range(blocks)]
    for b in range(blocks):
        at = slice(b * TILE, (b + 1) * TILE)
        before = down[b - 1] if b > 0 else 0.0
        after = up[b + 1] if b + 1 < blocks else 0.0
        total = row(1, b) + gain * frame_ref[:, at].astype(F32)
        total = total + jnp.where(lane < ROW, before, down[b])
        total = total + jnp.where(lane >= TILE - ROW, after, up[b])
        out_ref[:, at] = jax.nn.gelu(total).astype(BF)


Z_ORDER = [5, 1, 7, 3, 4, 2, 6, 0]
Y_ORDER = [4, 2, 6, 1, 5, 3, 7, 0]
X_ORDER = [5, 7, 1, 3, 4, 6, 0, 2]
S_ORDER = [i * 8 + k for ks in ([4, 6, 5, 3, 7], [2, 1, 0]) for i in [5, 7, 0, 2, 4, 6, 1, 3] for k in ks]


def exchange(x, axis, order):
    return lax.all_to_all(x, axis, 0, 0, axis_index_groups=[order], tiled=True)


def body(groups, frames, decay_rate, step_size, in_kernel, out_kernel, skip_gain):
    _, channels, cells = frames.shape
    blocks = cells // TILE
    states = in_kernel.shape[1]
    members = lax.axis_size("xc")
    part = states // members
    frame = frames.reshape(channels, cells)
    shape = jax.ShapeDtypeStruct
    rates = decay_rate.shape[0]
    step = call(
        lay_step,
        shape((8, TILE), F32),
        step_size,
        places=(pltpu.SMEM,),
        cost=pl.CostEstimate(flops=10**9, bytes_accessed=0, transcendentals=0),
    )
    cut = call(
        functools.partial(cut_rows, Z_ORDER),
        shape((blocks, channels + channels // 2 + 8, TILE), BF),
        step,
        frame,
        decay_rate[None],
        cost=pl.CostEstimate(flops=10**9, bytes_accessed=0, transcendentals=0),
    )
    rows = exchange(cut, "chan", Z_ORDER)
    driven = call(
        functools.partial(drive, Z_ORDER, X_ORDER),
        shape((members, part + 8, TILE), BF),
        rows,
        in_kernel,
    )
    driven = exchange(driven, "xc", X_ORDER)
    final = call(functools.partial(finish_group, X_ORDER), shape((groups, part + 8, TILE), BF), driven)
    final = exchange(final, "y", Y_ORDER)
    state = call(
        functools.partial(run_group, Y_ORDER, X_ORDER, S_ORDER),
        shape((members * blocks, part, TILE), BF),
        final,
        driven,
    )
    state = exchange(state, ("xc", "chan"), S_ORDER)
    out = call(
        functools.partial(finish, S_ORDER),
        shape((channels, cells), BF),
        state,
        frame,
        out_kernel,
        skip_gain[None],
    )
    return out[None]


def solution(mesh):
    groups, members = 8, 8
    fine = Mesh(mesh.devices.reshape(groups, members, mesh.shape["chan"]), ("y", "xc", "chan"))
    time = ("y", "xc")
    in_specs = (P(time, "chan", None), P("chan"), P(time), P(), P(None, "chan", None), P("chan"))
    out_specs = P(time, "chan", None)
    return jax.shard_map(
        functools.partial(body, groups), mesh=fine, in_specs=in_specs, out_specs=out_specs, check_vma=False
    )
```

```python
import functools

import jax
import jax.numpy as jnp
from jax import lax
from jax.experimental import pallas as pl
from jax.experimental.pallas import tpu as pltpu
from jax.sharding import Mesh, PartitionSpec as P

ROW = 32
TILE = 128
BF = jnp.bfloat16
F32 = jnp.float32


def lanes_of(shape):
    return lax.broadcasted_iota(jnp.int32, shape, len(shape) - 1)


def roll_lanes(x, by):
    return pltpu.roll(x, by % x.shape[-1], len(x.shape) - 1)


def to_column(row):
    n = row.shape[-1]
    eye = lax.broadcasted_iota(jnp.int32, (n, n), 0) == lax.broadcasted_iota(jnp.int32, (n, n), 1)
    return jnp.sum(jnp.where(eye, jnp.broadcast_to(row, (n, n)), 0.0), axis=1, keepdims=True)


def pieces(column):
    high = column.astype(BF).astype(F32)
    rest = column - high
    mid = rest.astype(BF).astype(F32)
    return high, mid, rest - mid


def spread(column, at, shape):
    lane = lanes_of(shape)
    tile = jnp.zeros(shape, F32)
    for n, piece in enumerate(pieces(column)):
        tile = jnp.where(lane == at + n, piece, tile)
    return tile


def collect(tile, at):
    lane = lanes_of(tile.shape)
    inside = (lane >= at) & (lane < at + 3)
    return jnp.sum(jnp.where(inside, tile.astype(F32), 0.0), axis=-1, keepdims=True)


def diagonal(n):
    return lax.broadcasted_iota(jnp.int32, (n, TILE), 0) == lanes_of((n, TILE))


def lay_rows(column):
    n = column.shape[0]
    at = lax.broadcasted_iota(jnp.int32, (8, TILE), 0)
    tile = jnp.zeros((8, TILE), F32)
    for r, piece in enumerate(pieces(column)):
        row = jnp.sum(jnp.where(diagonal(n), piece, 0.0), axis=0, keepdims=True)
        tile = jnp.where(at == r, row, tile)
    return tile.astype(BF)


def read_rows(tile, n):
    row = jnp.sum(tile.astype(F32), axis=0, keepdims=True)
    return jnp.sum(jnp.where(diagonal(n), row, 0.0), axis=1, keepdims=True)


def call(kernel, outs, *operands, places=None, out_place=pltpu.VMEM, scratch=(), vmem=32, cost=None):
    places = places or (pltpu.VMEM,) * len(operands)
    specs = [pl.BlockSpec(memory_space=place) for place in places]
    return pl.pallas_call(
        kernel,
        out_shape=outs,
        in_specs=specs,
        out_specs=pl.BlockSpec(memory_space=out_place),
        scratch_shapes=scratch,
        cost_estimate=cost,
        compiler_params=pltpu.CompilerParams(vmem_limit_bytes=vmem << 20),
    )(*operands)


def lay_step(step_ref, out_ref):
    out_ref[...] = jnp.full(out_ref.shape, step_ref[0], F32)


def cut_rows(order, step_ref, frame_ref, rate_ref, out_ref):
    blocks = out_ref.shape[0]
    channels = frame_ref.shape[0]
    half = channels // 2
    lane = lanes_of((channels, TILE))
    after_at, before_at = lane < ROW, lane >= TILE - ROW
    near = lane[:half]
    outer = (near < ROW) | (near >= TILE - ROW)
    rate = to_column(rate_ref[...])
    at = lax.broadcasted_iota(jnp.int32, (8, TILE), 0)
    meta = lay_rows(rate).astype(F32)
    for r, piece in enumerate(pieces(step_ref[:1])):
        meta = jnp.where(at == r + 3, piece, meta)
    meta = meta.astype(BF)
    for at, b in enumerate(order):
        out_ref[at, :channels] = frame_ref[:, b * TILE : (b + 1) * TILE]
        side = jnp.zeros((channels, TILE), F32)
        if b + 1 < blocks:
            after = frame_ref[:, (b + 1) * TILE : (b + 2) * TILE].astype(F32)
            side = jnp.where(after_at, after, side)
        if b > 0:
            before = frame_ref[:, (b - 1) * TILE : b * TILE].astype(F32)
            side = jnp.where(before_at, before, side)
        packed = jnp.where(outer, side[:half], roll_lanes(side[half:], TILE // 2))
        out_ref[at, channels : channels + half] = packed.astype(BF)
        out_ref[at, channels + half :] = meta


def drive(order, part_order, rows_ref, weight_ref, out_ref):
    blocks, height, _ = rows_ref.shape
    states, depth = weight_ref.shape[1:]
    channels = depth // blocks
    half = channels // 2
    main = jnp.concatenate([rows_ref[order.index(b), :channels] for b in range(blocks)], axis=0)
    sides = []
    rates = []
    for b in range(blocks):
        at = order.index(b)
        packed = rows_ref[at, channels : channels + half]
        sides += [packed, roll_lanes(packed.astype(F32), TILE // 2).astype(BF)]
        meta = rows_ref[at, channels + half :]
        rates.append(read_rows(meta[:3], states // blocks))
    side = jnp.concatenate(sides, axis=0)
    step = jnp.sum(rows_ref[0, channels + half + 3 : channels + half + 6].astype(F32), axis=0, keepdims=True)[:, :1]
    lane = lanes_of(main.shape)
    column = lanes_of((states, TILE)) % ROW
    total = None
    for i in range(3):
        if i == 0:
            source = jnp.where(lane >= TILE - ROW, side, main)
        elif i == 2:
            source = jnp.where(lane < ROW, side, main)
        else:
            source = main
        weight = weight_ref[3 * i : 3 * i + 3].reshape(3 * states, depth)
        left, row, right = jnp.split(jnp.dot(weight, source, preferred_element_type=F32), 3)
        row = row + jnp.where(column > 0, roll_lanes(left, 1), 0.0)
        row = row + jnp.where(column < ROW - 1, roll_lanes(right, -1), 0.0)
        row = roll_lanes(row, (1 - i) * ROW) if i != 1 else row
        total = row if total is None else total + row
    decay = jnp.exp(-jnp.concatenate(rates, axis=0) * step)
    inject = jnp.sqrt(1.0 - decay * decay)
    scaled = (inject * total).astype(BF)
    part = states // len(part_order)
    for at, g in enumerate(part_order):
        out_ref[at, :part] = scaled[g * part : (g + 1) * part]
        out_ref[at, part:] = lay_rows(decay[g * part : (g + 1) * part])


def finish_group(order, driven_ref, out_ref):
    frames, height, _ = driven_ref.shape
    part = height - 8
    state = None
    through = None
    for f in range(frames):
        at = order.index(f)
        decay = read_rows(driven_ref[at, part:], part)
        value = driven_ref[at, :part].astype(F32)
        state = value if f == 0 else decay * state + value
        through = decay if f == 0 else decay * through
    final = state.astype(BF)
    meta = lay_rows(through)
    for g in range(out_ref.shape[0]):
        out_ref[g, :part] = final
        out_ref[g, part:] = meta


def run_group(order, frame_order, spread_order, final_ref, driven_ref, out_ref):
    groups = final_ref.shape[0]
    frames, height, _ = driven_ref.shape
    part = height - 8
    at = lax.axis_index("y")
    state = jnp.zeros((part, TILE), F32)
    for g in range(groups):
        source = order.index(g)
        through = read_rows(final_ref[source, part:], part)
        moved = through * state + final_ref[source, :part].astype(F32)
        state = jnp.where(g < at, moved, state)
    copies = out_ref.shape[0] // frames
    for f in range(frames):
        source = frame_order.index(f)
        decay = read_rows(driven_ref[source, part:], part)
        state = decay * state + driven_ref[source, :part].astype(F32)
        rounded = state.astype(BF)
        for c in range(copies):
            out_ref[spread_order.index(f * copies + c)] = rounded


def finish(order, state_ref, frame_ref, weight_ref, gain_ref, out_ref, done_ref, sems):
    channels, cells = frame_ref.shape
    blocks = cells // TILE
    states = weight_ref.shape[2]
    parts = len(order) // blocks

    def rows(b):
        return jnp.concatenate([state_ref[order.index(p * blocks + b)] for p in range(parts)], axis=0)

    source = jnp.concatenate([rows(b) for b in range(blocks)], axis=1)
    gains = to_column(gain_ref[...])
    halves = 2
    channels //= halves
    copies = []
    for half in range(halves):
        top = half * channels
        weight = weight_ref[:, top : top + channels].reshape(9 * channels, states)
        taps = jnp.dot(weight, source, preferred_element_type=F32)
        lane = lanes_of((channels, TILE))
        column = lane % ROW
        gain = gains[top : top + channels]

        def row(i, b):
            def tap(j):
                at = (3 * i + j) * channels
                return taps[at : at + channels, b * TILE : (b + 1) * TILE]

            left = jnp.where(column > 0, roll_lanes(tap(0), 1), 0.0)
            right = jnp.where(column < ROW - 1, roll_lanes(tap(2), -1), 0.0)
            return tap(1) + left + right

        down = [roll_lanes(row(0, b), ROW) for b in range(blocks)]
        up = [roll_lanes(row(2, b), -ROW) for b in range(blocks)]
        for b in range(blocks):
            at = slice(b * TILE, (b + 1) * TILE)
            before = down[b - 1] if b > 0 else 0.0
            after = up[b + 1] if b + 1 < blocks else 0.0
            total = row(1, b) + gain * frame_ref[top : top + channels, at].astype(F32)
            total = total + jnp.where(lane < ROW, before, down[b])
            total = total + jnp.where(lane >= TILE - ROW, after, up[b])
            done_ref[top : top + channels, at] = jax.nn.gelu(total).astype(BF)
        rows_at = pl.ds(top, channels)
        copies.append(pltpu.make_async_copy(done_ref.at[rows_at], out_ref.at[rows_at], sems.at[half]))
        copies[-1].start()
    for copy in copies:
        copy.wait()


Z_ORDER = [5, 1, 7, 3, 4, 2, 6, 0]
Y_ORDER = [4, 2, 6, 1, 5, 3, 7, 0]
X_ORDER = [5, 7, 1, 3, 4, 6, 0, 2]
S_ORDER = [i * 8 + k for ks in ([4, 6, 5, 3, 7], [2, 1, 0]) for i in [5, 7, 0, 2, 4, 6, 1, 3] for k in ks]


def exchange(x, axis, order):
    return lax.all_to_all(x, axis, 0, 0, axis_index_groups=[order], tiled=True)


def body(groups, frames, decay_rate, step_size, in_kernel, out_kernel, skip_gain):
    _, channels, cells = frames.shape
    blocks = cells // TILE
    states = in_kernel.shape[1]
    members = lax.axis_size("xc")
    part = states // members
    frame = frames.reshape(channels, cells)
    shape = jax.ShapeDtypeStruct
    rates = decay_rate.shape[0]
    step = call(
        lay_step,
        shape((8, TILE), F32),
        step_size,
        places=(pltpu.SMEM,),
        cost=pl.CostEstimate(flops=10**9, bytes_accessed=0, transcendentals=0),
    )
    cut = call(
        functools.partial(cut_rows, Z_ORDER),
        shape((blocks, channels + channels // 2 + 8, TILE), BF),
        step,
        frame,
        decay_rate[None],
        cost=pl.CostEstimate(flops=10**9, bytes_accessed=0, transcendentals=0),
    )
    rows = exchange(cut, "chan", Z_ORDER)
    driven = call(
        functools.partial(drive, Z_ORDER, X_ORDER),
        shape((members, part + 8, TILE), BF),
        rows,
        in_kernel,
    )
    driven = exchange(driven, "xc", X_ORDER)
    final = call(functools.partial(finish_group, X_ORDER), shape((groups, part + 8, TILE), BF), driven)
    final = exchange(final, "y", Y_ORDER)
    state = call(
        functools.partial(run_group, Y_ORDER, X_ORDER, S_ORDER),
        shape((members * blocks, part, TILE), BF),
        final,
        driven,
    )
    state = exchange(state, ("xc", "chan"), S_ORDER)
    out = call(
        functools.partial(finish, S_ORDER),
        shape((channels, cells), BF),
        state,
        frame,
        out_kernel,
        skip_gain[None],
        out_place=pltpu.HBM,
        scratch=(pltpu.VMEM((channels, cells), BF), pltpu.SemaphoreType.DMA((2,))),
    )
    return out[None]


def solution(mesh):
    groups, members = 8, 8
    fine = Mesh(mesh.devices.reshape(groups, members, mesh.shape["chan"]), ("y", "xc", "chan"))
    time = ("y", "xc")
    in_specs = (P(time, "chan", None), P("chan"), P(time), P(), P(None, "chan", None), P("chan"))
    out_specs = P(time, "chan", None)
    return jax.shard_map(
        functools.partial(body, groups), mesh=fine, in_specs=in_specs, out_specs=out_specs, check_vma=False
    )
```
